256 devices in a mesh: section: 4 (over x_hi, core), dp: 64 (over z, x_lo, y).
Axes of the slice: x: 4 (x_hi: 2, x_lo: 2; x = x_hi * 2 + x_lo), y: 4, z: 8, core: 2. Of those that a mesh axis runs over, the one named last changes fastest.
Arguments:
- encoder_states: bfloat16 [2, 2048, 2048], P(None, 'dp', 'section'), may hold values from -860 to 860
- encoder_lengths: int32 [2, 64], P(None, 'dp'), may hold values from 8 to 32, as said below
- final_gain: bfloat16 [2048], P('section'), may hold values from 0.25 to 1.75
- decoder_states: bfloat16 [2, 4096, 2048], P(None, 'dp'), may hold values from -1800 to 1800
- query_gain: bfloat16 [4, 2048], P('section'), may hold values from 0.25 to 1.75
- cross_weight: bfloat16 [4, 2048, 4096], P('section', 'dp'), may hold values from -1 to 1.02
- upstream: bfloat16 [2, 4096, 2048], P(None, 'dp'), may hold values from -6 to 6
Outputs:
- encoder_gradient: float32 [2, 2048, 2048], P(None, 'dp', 'section')
- final_gradient: float32 [2048], P('section')
- layers_gradient: float32 [4, 2048], P('section')
The draws below stay inside these ranges and needn't reach their ends.
Inputs may be any that keep to these rules, and one draw needn't show every extreme that they name: `encoder_lengths`: the valid positions of a sequence are its first ones; in each micro-batch some sequence has all 32.
All inputs are finite; a program needn't handle non-finite values.
Results may differ from the reference program's by a relative error of at most 0.013.
The reference program's roundings to bfloat16 on the way (of `encoder_out`, `pair_rows`, `queries`, `rounded`, `stream`, `incoming_heads`, `score_gradient` and `pair_gradient`) count: a program that leaves them out, or rounds other values in their place, can miss the bound.
Values may be sent and summed in bfloat16 or wider, within the bound.
No kernel may reach another device: no remote copies, remote signals or barrier semaphores. Data moves between devices by JAX's collectives and lax.ppermute only.
A program may use at most 128 MiB of HBM per device.

```python
import math
import jax
import jax.numpy as jnp
from jax import lax

D = 2048
HEADS = 32
HEAD = 64
MICRO = 2
ENC_LEN = 32
DEC_LEN = 64
INNER = 2048
SEQS = 64
LAYERS = 4


def draw_encoder_states(key, part):
    key = jax.random.fold_in(key, 11)
    noise_key, scale_key, column_key = jax.random.split(key, 3)
    array_shape = (MICRO, SEQS * ENC_LEN, D)
    base_values = jnp.clip(jax.random.normal(noise_key, array_shape), -6.0, 6.0)
    row_scale = jnp.exp(jax.random.uniform(scale_key, (MICRO, SEQS * ENC_LEN, 1)) * math.log(10.0))
    columns = jnp.exp(math.log(10.0) * jnp.arange(D) / D + jax.random.uniform(column_key, (D,), minval=-0.35, maxval=0.35))
    values = base_values * row_scale * columns
    return values.astype(jnp.bfloat16)


def draw_decoder_states(key, part):
    key = jax.random.fold_in(key, 12)
    noise_key, scale_key, column_key = jax.random.split(key, 3)
    array_shape = (MICRO, SEQS * DEC_LEN, D)
    base_values = jnp.clip(jax.random.normal(noise_key, array_shape), -6.0, 6.0)
    row_order = jnp.arange(SEQS * DEC_LEN) / (SEQS * DEC_LEN)
    row_scale = jnp.exp(jax.random.uniform(scale_key, (MICRO, SEQS * DEC_LEN, 1)) * math.log(10.0)) * jnp.exp(math.log(3.0) * row_order)[None, :, None]
    columns = jnp.exp(jax.random.uniform(column_key, (D,)) * math.log(10.0))
    values = base_values * row_scale * columns
    return values.astype(jnp.bfloat16)


def draw_encoder_lengths(key, part):
    key = jax.random.fold_in(key, 13)
    length_key, full_key = jax.random.split(key, 2)
    lengths = jax.random.randint(length_key, (MICRO, SEQS), ENC_LEN // 4, ENC_LEN + 1)
    full_index = jax.random.randint(full_key, (MICRO, 1), 0, SEQS)
    return jnp.where(jnp.arange(SEQS)[None, :] == full_index, ENC_LEN, lengths).astype(jnp.int32)


def draw_cross_weight(key, part):
    key = jax.random.fold_in(key, 14)
    array_shape = (LAYERS, D, 2 * INNER)
    base_values = jnp.clip(jax.random.normal(key, array_shape), -6.0, 6.0) / math.sqrt(D)
    return base_values.astype(jnp.bfloat16)


def block_levels(stream_key, shape, cuts, least, high):
    gain, own = 1.0, jax.random.fold_in(stream_key, 6)
    for dim, blocks in cuts:
        draws = jnp.exp(jax.random.uniform(jax.random.fold_in(own, dim), (blocks,), jnp.float32, least / len(cuts), high / len(cuts)))
        gain = gain * jnp.repeat(draws, shape[dim] // blocks).reshape([-1 if axis == dim else 1 for axis in range(len(shape))])
    return gain


def scatter_about(key, shape, deviation, reach, cuts=(), kind=jnp.bfloat16):
    loudness = block_levels(key, shape, cuts, -0.22, 0.18) if cuts else 1.0
    entries = jax.random.normal(key, shape, jnp.float32) * deviation * loudness
    return jnp.minimum(jnp.maximum(entries, -reach), reach).astype(kind)


def setup_inputs(seed: int = 0) -> dict:
    splits = jax.random.split(jax.random.key(seed), 8)
    return {
        "encoder_states": draw_encoder_states(jax.random.fold_in(splits[7], 71), 0),
        "encoder_lengths": draw_encoder_lengths(jax.random.fold_in(splits[7], 71), 0),
        "final_gain": jnp.clip(1.0 + 0.15 * jax.random.normal(splits[2], (D,), jnp.float32), 0.25, 1.75).astype(jnp.bfloat16),
        "decoder_states": draw_decoder_states(jax.random.fold_in(splits[7], 71), 0),
        "query_gain": jnp.clip(1.0 + 0.15 * jax.random.normal(splits[4], (LAYERS, D), jnp.float32), 0.25, 1.75).astype(jnp.bfloat16),
        "cross_weight": draw_cross_weight(jax.random.fold_in(splits[7], 71), 0),
        "upstream": scatter_about(splits[6], (MICRO, SEQS * DEC_LEN, D), 1.0, 6.0, ((1, 64),)),
    }


EPSILON = 1e-06

def rms_factor(matrix):
    return lax.rsqrt(lax.optimization_barrier(jnp.mean(matrix * matrix, axis=-1, keepdims=True)) + EPSILON)

def widened(matrix):
    return lax.optimization_barrier(matrix).astype(jnp.float32)

def heads_of(matrix, length):
    return widened(matrix).reshape(matrix.shape[0], -1, length, HEADS, HEAD)

def attend_parts(stream, gain_row, key_rows, allowed):
    stream_wide = widened(stream)
    factor = rms_factor(stream_wide)
    queries = (stream_wide * factor * gain_row.astype(jnp.float32)).astype(jnp.bfloat16)
    scores = jnp.einsum('mbqhe,mbkhe->mbhqk', heads_of(queries, DEC_LEN), heads_of(key_rows, ENC_LEN)) * HEAD ** (-0.5)
    visible = allowed[:, :, None, None, :]
    scores = jnp.where(visible, scores, -1e+30)
    highest = lax.optimization_barrier(jnp.max(scores, axis=-1, keepdims=True))
    weights = jnp.where(visible, jnp.exp(scores - highest), 0.0)
    softmax_rows = weights / lax.optimization_barrier(jnp.sum(weights, axis=-1, keepdims=True))
    return (stream_wide, factor, queries, softmax_rows)

def reference(encoder_states, encoder_lengths, final_gain, decoder_states, query_gain, cross_weight, upstream):
    states_wide = encoder_states.astype(jnp.float32)
    encoder_factor = rms_factor(states_wide)
    encoder_out = (states_wide * encoder_factor * final_gain.astype(jnp.float32)).astype(jnp.bfloat16)
    micro_count, encoder_rows, model_width = encoder_out.shape
    inner_width = HEADS * HEAD
    allowed = jnp.arange(ENC_LEN)[None, None, :] < encoder_lengths[:, :, None]
    flat_out = encoder_out.reshape(-1, model_width)
    saved_layers = []
    stream = decoder_states
    for layer_index in range(LAYERS):
        pair_rows = jnp.dot(flat_out, cross_weight[layer_index], preferred_element_type=jnp.float32).astype(jnp.bfloat16)
        pair_rows = pair_rows.reshape(micro_count, encoder_rows, 2 * inner_width)
        key_rows = pair_rows[..., :inner_width]
        value_rows = pair_rows[..., inner_width:]
        saved_layers.append((stream, key_rows, value_rows))
        stream_wide, factor, queries, softmax_rows = attend_parts(stream, query_gain[layer_index], key_rows, allowed)
        rounded = widened(softmax_rows.astype(jnp.bfloat16))
        context = jnp.einsum('mbhqk,mbkhe->mbqhe', rounded, heads_of(value_rows, ENC_LEN))
        stream = (stream_wide + context.reshape(stream_wide.shape)).astype(jnp.bfloat16)
    incoming = upstream.astype(jnp.float32)
    encoder_terms = jnp.zeros(encoder_out.shape, jnp.float32)
    layer_gains = []
    head_scale = HEAD ** (-0.5)
    for layer_index in reversed(range(LAYERS)):
        stream, key_rows, value_rows = saved_layers[layer_index]
        layer_gain = query_gain[layer_index]
        stream_wide, factor, queries, softmax_rows = attend_parts(stream, layer_gain, key_rows, allowed)
        rounded = widened(softmax_rows.astype(jnp.bfloat16))
        incoming_heads = heads_of(incoming.astype(jnp.bfloat16), DEC_LEN)
        value_heads = heads_of(value_rows, ENC_LEN)
        softmax_gradient = jnp.einsum('mbqhe,mbkhe->mbhqk', incoming_heads, value_heads)
        value_gradient = jnp.einsum('mbhqk,mbqhe->mbkhe', rounded, incoming_heads)
        score_gradient = softmax_rows * (softmax_gradient - lax.optimization_barrier(jnp.sum(softmax_rows * softmax_gradient, axis=-1, keepdims=True)))
        score_gradient = widened(score_gradient.astype(jnp.bfloat16))
        query_gradient = jnp.einsum('mbhqk,mbkhe->mbqhe', score_gradient, heads_of(key_rows, ENC_LEN)) * head_scale
        key_gradient = jnp.einsum('mbhqk,mbqhe->mbkhe', score_gradient, heads_of(queries, DEC_LEN)) * head_scale
        pair_gradient = jnp.concatenate([key_gradient.reshape(micro_count, encoder_rows, inner_width), value_gradient.reshape(micro_count, encoder_rows, inner_width)], axis=-1).astype(jnp.bfloat16)
        encoder_terms = encoder_terms + jnp.dot(pair_gradient.reshape(-1, 2 * inner_width), cross_weight[layer_index].T, preferred_element_type=jnp.float32).reshape(encoder_out.shape)
        query_gradient = query_gradient.reshape(stream_wide.shape)
        scaled = query_gradient * layer_gain.astype(jnp.float32)
        layer_gains.append(lax.optimization_barrier(jnp.sum(query_gradient * stream_wide * factor, axis=(0, 1))))
        incoming = incoming + factor * scaled - stream_wide * factor ** 3 * lax.optimization_barrier(jnp.mean(scaled * stream_wide, axis=-1, keepdims=True))
    layers_gradient = jnp.stack(layer_gains[::-1])
    scaled = encoder_terms * final_gain.astype(jnp.float32)
    encoder_gradient = encoder_factor * scaled - states_wide * encoder_factor ** 3 * lax.optimization_barrier(jnp.mean(scaled * states_wide, axis=-1, keepdims=True))
    final_gradient = lax.optimization_barrier(jnp.sum(encoder_terms * states_wide * encoder_factor, axis=(0, 1)))
    return (encoder_gradient, final_gradient, layers_gradient)
```

```python
import jax
import jax.numpy as jnp
from jax import lax
from jax.experimental import pallas as pl
from jax.experimental.pallas import tpu as pltpu
from jax.sharding import PartitionSpec as P

D = 2048
HEAD = 64
ENC = 32
ROWS = 32
LAYERS = 4
GROUPS = 8
EPSILON = 1e-06
AXES = ("section", "dp")
NY, NZ = 4, 8
BF, F32 = jnp.bfloat16, jnp.float32
MIB = 1 << 20


def shift(block, dxh=0, dc=0, dz=0, dxl=0, dy=0):
    pairs = []
    for i in range(256):
        xh, c, z, xl, y = i >> 7, (i >> 6) & 1, (i >> 3) & 7, (i >> 2) & 1, i & 3
        to = ((xh ^ dxh) << 7) | ((c ^ dc) << 6) | (((z + dz) % NZ) << 3) | ((xl ^ dxl) << 2) | ((y + dy) % NY)
        pairs.append((i, to))
    return lax.ppermute(block, AXES, pairs)


def kernel_call(body, ids, operands, outs, scratch=(), limit=24, cost=None):
    return pl.pallas_call(
        body,
        out_shape=[jax.ShapeDtypeStruct(s, d) for s, d in outs],
        in_specs=[pl.BlockSpec(memory_space=pltpu.SMEM)] + [pl.BlockSpec(memory_space=pltpu.VMEM)] * len(operands),
        out_specs=[pl.BlockSpec(memory_space=pltpu.VMEM)] * len(outs),
        scratch_shapes=[pltpu.VMEM(s, d) for s, d in scratch],
        compiler_params=pltpu.CompilerParams(vmem_limit_bytes=limit * MIB),
    )(ids, *operands)


def lanes(start, size):
    return pl.ds(pl.multiple_of(start, size), size)


PLANE = [(dxl, dy) for dxl in range(2) for dy in range(NY)]


def prepare_body(ids, weight, states, final_gain, query_gain, *outs):
    xl, y = ids[3], ids[4]
    for k, (dxl, dy) in enumerate(PLANE):
        column = 2 * ((y + dy) % NY) + (xl + dxl) % 2
        outs[k][...] = weight[:, lanes(column * 512, 512)]
    pack = outs[8]
    pack[:64, :] = states[...]
    gains = [final_gain[...].astype(F32)]
    gains += [query_gain[:, i * 512 : (i + 1) * 512].astype(F32) for i in range(4)]
    gains += [jnp.zeros((11, 512), F32)]
    pack[64:, :] = jnp.concatenate(gains, axis=0).astype(BF)


def gather_rows_body(ids, *refs):
    xl, y = ids[3], ids[4]
    out = refs[8]
    for k, (dxl, dy) in enumerate(PLANE):
        row = ((xl + dxl) % 2) * 4 + (y + NY - dy) % NY
        out[lanes(row * 32, 32), :] = refs[k][...]


def norm_body(ids, p0, p1, p2, p3, encoder_out, factor, query_gains, final_gains, wide):
    section = ids[0] * 2 + ids[1]
    for j, pack in enumerate((p0, p1, p2, p3)):
        peer = section ^ j
        wide[:, lanes(peer * 512, 512)] = pack[:64, :].astype(F32)
        gains = pack[64:, :].astype(F32)
        final_gains[:, lanes(peer * 512, 512)] = gains[0:1]
        for i in range(4):
            query_gains[peer, :, i * 512 : (i + 1) * 512] = gains[1 + i : 2 + i]
    states = wide[...]
    scale = lax.rsqrt(jnp.mean(states * states, axis=-1, keepdims=True) + EPSILON)
    factor[...] = jnp.broadcast_to(scale, (64, 128))
    encoder_out[...] = (states * scale * final_gains[...]).astype(BF)


def project_body(ids, *refs):
    xh, z = ids[0], ids[2]
    rows, blocks, outs, weight, held = refs[:8], refs[8:16], refs[16:32], refs[32], refs[33]
    for k in range(8):
        held[k * 64 : (k + 1) * 64, :] = rows[k][...]
    for k, dz in enumerate(RING):
        weight[lanes(((z + NZ + dz) % NZ) * 256, 256), :] = blocks[k][...]
    pair_rows = jnp.dot(held[...], weight[...], preferred_element_type=F32).astype(BF)
    for k in range(8):
        first = pair_rows[k * 64 : k * 64 + 32]
        second = pair_rows[k * 64 + 32 : k * 64 + 64]
        outs[2 * k][...] = jnp.where(xh == 0, first, second)
        outs[2 * k + 1][...] = jnp.where(xh == 0, second, first)


RING = (0, -1, -2, -3, 1, 2, 3, -4)


def collect_body(ids, *refs):
    xh, xl, y = ids[0], ids[3], ids[4]
    out = refs[16]
    for k, (dxl, dy) in enumerate(PLANE):
        column = 2 * ((y + dy) % NY) + (xl + dxl) % 2
        for dm in range(2):
            out[(xh + dm) % 2, :, lanes(column * 512, 512)] = refs[2 * k + dm][...]


def decoder_body(ids, own, other, stream_in, upstream, query_gains, keep, send, gain_parts,
                 pairs, streams, queries, softmax, incoming, query_gradient, gradients):
    xh, c = ids[0], ids[1]
    length = jnp.where(xh == 0, ids[5], ids[6])
    for i in range(2):
        pairs[2 * i + c] = own[i]
        pairs[2 * i + 1 - c] = other[i]
    streams[0] = stream_in[...]
    incoming[...] = upstream[...].astype(F32)
    block = (lax.broadcasted_iota(jnp.int32, (128, 256), 0) // 32) == (
        lax.broadcasted_iota(jnp.int32, (128, 256), 1) // HEAD
    )
    block = jnp.where(block, 1.0, 0.0).astype(BF)
    lane = lax.broadcasted_iota(jnp.int32, (ROWS, 256), 1)
    visible = lax.broadcasted_iota(jnp.int32, (ENC, 128), 0) < length
    scale = HEAD**-0.5

    def spread(part):
        return jnp.concatenate([part] * 4, axis=0) * block

    def fold(part):
        low = jnp.where(lane < 64, part[0:32], part[32:64])
        high = jnp.where(lane < 192, part[64:96], part[96:128])
        return jnp.where(lane < 128, low, high)

    def dot(a, b, dims):
        return lax.dot_general(a, b, (dims, ((), ())), preferred_element_type=F32)

    def forward(layer, carry):
        wide = streams[layer].astype(F32)
        factor = lax.rsqrt(jnp.mean(wide * wide, axis=-1, keepdims=True) + EPSILON)
        queries[layer] = (wide * factor * query_gains[layer]).astype(BF)
        for g in range(GROUPS):
            span = slice(g * 256, (g + 1) * 256)
            keys = pairs[layer, :, span]
            values = pairs[layer, :, D + g * 256 : D + (g + 1) * 256]
            scores = dot(keys, spread(queries[layer, :, span]), ((1,), (1,))) * scale
            scores = jnp.where(visible, scores, -1e30)
            highest = jnp.max(scores, axis=0, keepdims=True)
            weights = jnp.where(visible, jnp.exp(scores - highest), 0.0)
            rows = weights / jnp.sum(weights, axis=0, keepdims=True)
            softmax[layer, g] = rows
            context = fold(dot(rows.astype(BF), values, ((0,), (0,))))
            streams[layer + 1, :, span] = (wide[:, span] + context).astype(BF)
        return carry

    lax.fori_loop(0, LAYERS, forward, 0)

    def backward(turn, carry):
        layer = LAYERS - 1 - turn
        wide = streams[layer].astype(F32)
        factor = lax.rsqrt(jnp.mean(wide * wide, axis=-1, keepdims=True) + EPSILON)
        for g in range(GROUPS):
            span = slice(g * 256, (g + 1) * 256)
            beyond = slice(D + g * 256, D + (g + 1) * 256)
            keys = pairs[layer, :, span]
            values = pairs[layer, :, beyond]
            rows = softmax[layer, g]
            heads = spread(incoming[:, span].astype(BF))
            softmax_gradient = dot(values, heads, ((1,), (1,)))
            gradients[layer, :, beyond] = dot(rows.astype(BF), heads, ((1,), (0,))).astype(BF)
            score_gradient = rows * (
                softmax_gradient - jnp.sum(rows * softmax_gradient, axis=0, keepdims=True)
            )
            score_gradient = score_gradient.astype(BF)
            query_gradient[:, span] = fold(dot(score_gradient, keys, ((0,), (0,)))) * scale
            key_gradient = dot(score_gradient, spread(queries[layer, :, span]), ((1,), (0,)))
            gradients[layer, :, span] = (key_gradient * scale).astype(BF)
        gradient = query_gradient[...]
        scaled = gradient * query_gains[layer]
        mean = jnp.mean(scaled * wide, axis=-1, keepdims=True)
        incoming[...] = incoming[...] + factor * scaled - wide * (factor * factor * factor) * mean
        gain_parts[layer] = jnp.sum(gradient * wide * factor, axis=0, keepdims=True)
        return carry

    lax.fori_loop(0, LAYERS, backward, 0)
    for i in range(2):
        keep[i] = gradients[2 * i + c]
        send[i] = gradients[2 * i + 1 - c]


FLIPS = [(dxh, dy) for dxh in range(2) for dy in range(NY)]


def join_body(ids, keep, received, *outs):
    xh, y = ids[0], ids[4]
    for k, (dxh, dy) in enumerate(FLIPS):
        span = lanes(((y + dy) % NY) * 1024, 1024)
        layer = (xh + dxh) % 2
        total = keep[layer, :, span].astype(F32) + received[layer, :, span].astype(F32)
        outs[k][...] = total.astype(BF)


def back_body(ids, *refs):
    xh, c, xl = ids[0], ids[1], ids[3]
    section = 2 * xh + c
    blocks, rows = refs[0:8], refs[8:12]
    weight, partner, gain_parts = refs[12:15]
    keep, send = refs[15:17]
    sums = refs[17:21]
    gathered, terms, parts = refs[21:24]
    for k in range(8):
        gathered[k * 32 : (k + 1) * 32, :] = blocks[k][...]
    mine = gathered[:, lanes(xl * 512, 512)]
    theirs = gathered[:, lanes((1 - xl) * 512, 512)]
    for q in range(4):
        span = slice(q * 512, (q + 1) * 512)
        dims = (((1,), (1,)), ((), ()))
        terms[:, span] = lax.dot_general(mine, weight[span, :], dims, preferred_element_type=F32) + lax.dot_general(
            theirs, partner[span, :], dims, preferred_element_type=F32
        )
    for i in range(2):
        keep[:, i * 512 : (i + 1) * 512] = terms[:, lanes((2 * i + c) * 512, 512)]
        send[:, i * 512 : (i + 1) * 512] = terms[:, lanes((2 * i + 1 - c) * 512, 512)].astype(BF)
    total = jnp.zeros((1, D), F32)
    for k, (dxh, dy) in enumerate(FLIPS):
        m = (xh + dxh) % 2
        encoder_rows = rows[dy][lanes(m * 32, 32), :].astype(F32)
        total += jnp.sum(terms[k * 32 : (k + 1) * 32, :] * encoder_rows, axis=0, keepdims=True)
    parts[...] = total
    for j in range(4):
        peer = section ^ j
        sums[j][:, :D] = gain_parts[peer]
        sums[j][:, D:] = parts[:, lanes(peer * 512, 512)]


def merge_body(ids, keep, received, own, *outs):
    xh = ids[0]
    scratch = outs[7]
    scratch[...] = keep[...] + received[...].astype(F32)
    for k, (dxh, dy) in enumerate(FLIPS):
        span = lanes(((xh + dxh) % 2) * 512, 512)
        for m in range(2):
            row = ((xh + m) % 2) * 128 + dy * 32
            part = scratch[lanes(row, 32), span]
            if k == 0:
                own[m * 32 : (m + 1) * 32, :] = part
            else:
                outs[k - 1][m * 32 : (m + 1) * 32, :] = part.astype(BF)


def per_device(
    encoder_states, encoder_lengths, final_gain, decoder_states, query_gain, cross_weight, upstream
):
    section = lax.axis_index("section")
    dp = lax.axis_index("dp")
    xh, c, z, xl, y = section // 2, section % 2, dp // 8, (dp // 4) % 2, dp % 4
    ids = jnp.stack([xh, c, z, xl, y, encoder_lengths[0, 0], encoder_lengths[1, 0], 0]).astype(jnp.int32)
    states = encoder_states.reshape(64, 512)
    stream = lax.dynamic_slice(decoder_states, (xh, c * ROWS, 0), (1, ROWS, D))[0]
    incoming = lax.dynamic_slice(upstream, (xh, c * ROWS, 0), (1, ROWS, D))[0]

    prepared = kernel_call(
        prepare_body,
        ids,
        (cross_weight[0], states, final_gain[None], query_gain),
        [((32, 512), BF)] * 8 + [((80, 512), BF)],
    )
    pack = prepared[8]
    packs = [pack, shift(pack, dc=1), shift(pack, dxh=1), shift(pack, dxh=1, dc=1)]
    columns = [prepared[0]] + [
        shift(prepared[k], dxl=dxl, dy=dy) for k, (dxl, dy) in enumerate(PLANE) if k
    ]
    (block,) = kernel_call(gather_rows_body, ids, columns, [((256, 512), BF)])
    forth1, back1 = shift(block, dz=1), shift(block, dz=-1)
    forth2, back2 = shift(forth1, dz=1), shift(back1, dz=-1)
    forth3, back3 = shift(forth2, dz=1), shift(back2, dz=-1)
    forth4 = shift(forth3, dz=1)
    ring = [block, forth1, forth2, forth3, back1, back2, back3, forth4]

    encoder_out, factor, query_gains, final_gains = kernel_call(
        norm_body,
        ids,
        packs,
        [((64, D), BF), ((64, 128), F32), ((4, 1, D), F32), ((1, D), F32)],
        [((64, D), F32)],
    )
    rows = [encoder_out] + [
        shift(encoder_out, dxl=dxl, dy=dy) for k, (dxl, dy) in enumerate(PLANE) if k
    ]
    projected = kernel_call(
        project_body,
        ids,
        rows + ring,
        [((32, 512), BF)] * 16 + [((D, 512), BF)],
        [((512, D), BF)],
    )
    weight = projected[16]
    moved = []
    for k, (dxl, dy) in enumerate(PLANE):
        for dm in range(2):
            part = projected[2 * k + dm]
            moved.append(shift(part, dxh=dm, dxl=dxl, dy=-dy) if k + dm else part)
    (own_pairs,) = kernel_call(collect_body, ids, moved, [((2, 32, 4096), BF)])
    other_pairs = shift(own_pairs, dc=1)
    partner = shift(weight, dxl=1)
    keep, send, gain_parts = kernel_call(
        decoder_body,
        ids,
        (own_pairs, other_pairs, stream, incoming, query_gains),
        [((2, 32, 4096), BF), ((2, 32, 4096), BF), ((4, 1, D), F32)],
        [
            ((4, 32, 4096), BF),
            ((5, ROWS, D), BF),
            ((4, ROWS, D), BF),
            ((4, GROUPS, ENC, 128), F32),
            ((ROWS, D), F32),
            ((ROWS, D), F32),
            ((4, 32, 4096), BF),
        ],
    )
    joined = kernel_call(
        join_body, ids, (keep, shift(send, dc=1)), [((32, 1024), BF)] * 8
    )
    gathered = [joined[0]] + [
        shift(joined[k], dxh=dxh, dy=dy) for k, (dxh, dy) in enumerate(FLIPS) if k
    ]
    back = kernel_call(
        back_body,
        ids,
        gathered + rows[:4] + [weight, partner, gain_parts],
        [((256, 1024), F32), ((256, 1024), BF)] + [((1, D + 512), F32)] * 4,
        [((256, 1024), BF), ((256, D), F32), ((1, D), F32)],
    )
    term_keep, term_send, sums = back[0], back[1], back[2:]
    merged = kernel_call(
        merge_body,
        ids,
        (term_keep, shift(term_send, dc=1)),
        [((64, 512), F32)] + [((64, 512), BF)] * 7,
        [((256, 1024), F32)],
    )
    terms = merged[0]
    for k, (dxh, dy) in enumerate(FLIPS):
        if k:
            terms = terms + shift(merged[k], dxh=dxh, dy=-dy).astype(F32)
    wide = states.astype(F32)
    scaled = terms * final_gain.astype(F32)[None]
    row_part = jnp.sum(scaled * wide, axis=-1, keepdims=True)
    row_sum = row_part + shift(row_part, dc=1) + shift(row_part, dxh=1) + shift(row_part, dxh=1, dc=1)
    scale = factor[:, :1]
    gradient = scale * scaled - wide * (scale * scale * scale) * (row_sum / D)

    total = sums[0] + shift(sums[1], dc=1) + shift(sums[2], dxh=1) + shift(sums[3], dxh=1, dc=1)
    total = total + sum(shift(total, dz=dz) for dz in range(1, NZ))
    total = total + sum(shift(total, dxl=dxl, dy=dy) for k, (dxl, dy) in enumerate(PLANE) if k)
    final_gradient = total[0, D:] / final_gain.astype(F32)
    return (gradient.reshape(2, 32, 512), final_gradient, total[:, :D])


def solution(mesh):
    return jax.shard_map(
        per_device,
        mesh=mesh,
        in_specs=(
            P(None, "dp", "section"),
            P(None, "dp"),
            P("section"),
            P(None, "dp", None),
            P("section", None),
            P("section", "dp", None),
            P(None, "dp", None),
        ),
        out_specs=(P(None, "dp", "section"), P("section"), P("section", None)),
        check_vma=False,
    )
```

```python
import jax
import jax.numpy as jnp
import numpy as np
from jax import lax
from jax.experimental import pallas as pl
from jax.experimental.pallas import tpu as pltpu
from jax.sharding import Mesh
from jax.sharding import PartitionSpec as P

D = 2048
HEAD = 64
ENC = 32
ROWS = 32
LAYERS = 4
GROUPS = 8
EPSILON = 1e-06
AXES = ("xh", "core", "z", "xl", "y")
SIZES = (2, 2, 8, 2, 4)
NY = 4
BF, F32 = jnp.bfloat16, jnp.float32
MIB = 1 << 20


def shift(block, **moves):
    pairs = []
    for index in np.ndindex(*SIZES):
        to = list(index)
        for axis, by in moves.items():
            k = AXES.index(axis)
            to[k] = (index[k] + by) % SIZES[k] if axis == "y" else index[k] ^ by
        pairs.append((int(np.ravel_multi_index(index, SIZES)), int(np.ravel_multi_index(to, SIZES))))
    return lax.ppermute(block, AXES, pairs)


def kernel_call(body, ids, operands, outs, scratch=(), limit=24):
    return pl.pallas_call(
        body,
        out_shape=[jax.ShapeDtypeStruct(s, d) for s, d in outs],
        in_specs=[pl.BlockSpec(memory_space=pltpu.SMEM)] + [pl.BlockSpec(memory_space=pltpu.VMEM)] * len(operands),
        out_specs=[pl.BlockSpec(memory_space=pltpu.VMEM)] * len(outs),
        scratch_shapes=[pltpu.VMEM(s, d) for s, d in scratch],
        compiler_params=pltpu.CompilerParams(vmem_limit_bytes=limit * MIB),
    )(ids, *operands)


def lanes(start, size):
    return pl.ds(pl.multiple_of(start, size), size)


def pack_body(ids, states, final_gain, query_gain, pack):
    pack[:64, :] = states[...]
    gains = [final_gain[...].astype(F32)]
    gains += [query_gain[:, i * 512 : (i + 1) * 512].astype(F32) for i in range(4)]
    gains += [jnp.zeros((11, 512), F32)]
    pack[64:, :] = jnp.concatenate(gains, axis=0).astype(BF)


def norm_body(ids, p0, p1, p2, p3, half, factor, query_gains, wide, final_gains):
    section, c = ids[0] * 2 + ids[1], ids[1]
    for j, pack in enumerate((p0, p1, p2, p3)):
        peer = section ^ j
        wide[:, lanes(peer * 512, 512)] = pack[:64, :].astype(F32)
        gains = pack[64:, :].astype(F32)
        final_gains[:, lanes(peer * 512, 512)] = gains[0:1]
        for i in range(4):
            query_gains[peer, :, i * 512 : (i + 1) * 512] = gains[1 + i : 2 + i]
    states = wide[...]
    scale = lax.rsqrt(jnp.mean(states * states, axis=-1, keepdims=True) + EPSILON)
    factor[...] = jnp.broadcast_to(scale, (64, 128))
    wide[...] = states * scale * final_gains[...]
    half[...] = wide[lanes(c * 32, 32), :].astype(BF)


def project_body(ids, own, other, weight, out, result):
    c, xl, y = ids[1], ids[3], ids[4]
    for i, rows in enumerate((own, other)):
        m = (c + i) % 2
        result[...] = jnp.dot(rows[...].reshape(256, D), weight[...], preferred_element_type=F32).astype(BF)
        for dy in range(NY):
            for dxl in range(2):
                place = m * 8 + (xl + dxl) % 2 * 4 + (y + NY - dy) % NY
                k = dy * 2 + dxl
                out[place] = result[k * 32 : (k + 1) * 32, :]


def decoder_body(ids, own, other, stream_in, upstream, query_gains, keep, send, gain_parts,
                 pairs, streams, queries, softmax, incoming, query_gradient, gradients):
    xh, c = ids[0], ids[1]
    length = jnp.where(xh == 0, ids[5], ids[6])
    for i in range(2):
        for k in range(8):
            pairs[2 * i + c, :, k * 512 : (k + 1) * 512] = own[8 * i + k]
            pairs[2 * i + 1 - c, :, k * 512 : (k + 1) * 512] = other[8 * i + k]
    streams[0] = stream_in[...]
    incoming[...] = upstream[...].astype(F32)
    block = (lax.broadcasted_iota(jnp.int32, (128, 256), 0) // 32) == (
        lax.broadcasted_iota(jnp.int32, (128, 256), 1) // HEAD
    )
    block = jnp.where(block, 1.0, 0.0).astype(BF)
    lane = lax.broadcasted_iota(jnp.int32, (ROWS, 256), 1)
    visible = lax.broadcasted_iota(jnp.int32, (ENC, 128), 0) < length
    scale = HEAD**-0.5

    def spread(part):
        return jnp.concatenate([part] * 4, axis=0) * block

    def fold(part):
        low = jnp.where(lane < 64, part[0:32], part[32:64])
        high = jnp.where(lane < 192, part[64:96], part[96:128])
        return jnp.where(lane < 128, low, high)

    def dot(a, b, dims):
        return lax.dot_general(a, b, (dims, ((), ())), preferred_element_type=F32)

    def forward(layer, carry):
        wide = streams[layer].astype(F32)
        factor = lax.rsqrt(jnp.mean(wide * wide, axis=-1, keepdims=True) + EPSILON)
        queries[layer] = (wide * factor * query_gains[layer]).astype(BF)
        for g in range(GROUPS):
            span = slice(g * 256, (g + 1) * 256)
            keys = pairs[layer, :, span]
            values = pairs[layer, :, D + g * 256 : D + (g + 1) * 256]
            scores = dot(keys, spread(queries[layer, :, span]), ((1,), (1,))) * scale
            scores = jnp.where(visible, scores, -1e30)
            highest = jnp.max(scores, axis=0, keepdims=True)
            weights = jnp.where(visible, jnp.exp(scores - highest), 0.0)
            rows = weights / jnp.sum(weights, axis=0, keepdims=True)
            softmax[layer, g] = rows
            context = fold(dot(rows.astype(BF), values, ((0,), (0,))))
            streams[layer + 1, :, span] = (wide[:, span] + context).astype(BF)
        return carry

    lax.fori_loop(0, LAYERS, forward, 0)

    def backward(turn, carry):
        layer = LAYERS - 1 - turn
        wide = streams[layer].astype(F32)
        factor = lax.rsqrt(jnp.mean(wide * wide, axis=-1, keepdims=True) + EPSILON)
        for g in range(GROUPS):
            span = slice(g * 256, (g + 1) * 256)
            beyond = slice(D + g * 256, D + (g + 1) * 256)
            keys = pairs[layer, :, span]
            values = pairs[layer, :, beyond]
            rows = softmax[layer, g]
            heads = spread(incoming[:, span].astype(BF))
            softmax_gradient = dot(values, heads, ((1,), (1,)))
            gradients[layer, :, beyond] = dot(rows.astype(BF), heads, ((1,), (0,))).astype(BF)
            score_gradient = rows * (
                softmax_gradient - jnp.sum(rows * softmax_gradient, axis=0, keepdims=True)
            )
            score_gradient = score_gradient.astype(BF)
            query_gradient[:, span] = fold(dot(score_gradient, keys, ((0,), (0,)))) * scale
            key_gradient = dot(score_gradient, spread(queries[layer, :, span]), ((1,), (0,)))
            gradients[layer, :, span] = (key_gradient * scale).astype(BF)
        gradient = query_gradient[...]
        scaled = gradient * query_gains[layer]
        mean = jnp.mean(scaled * wide, axis=-1, keepdims=True)
        incoming[...] = incoming[...] + factor * scaled - wide * (factor * factor * factor) * mean
        gain_parts[layer] = jnp.sum(gradient * wide * factor, axis=0, keepdims=True)
        return carry

    lax.fori_loop(0, LAYERS, backward, 0)
    for i in range(2):
        keep[i] = gradients[2 * i + c]
        send[i] = gradients[2 * i + 1 - c]


def join_body(ids, keep, received, out):
    for xh in range(2):
        for y in range(NY):
            for half in range(2):
                span = slice(half * 2048 + y * 512, half * 2048 + (y + 1) * 512)
                total = keep[xh, :, span].astype(F32) + received[xh, :, span].astype(F32)
                out[xh * NY + y, :, half * 512 : (half + 1) * 512] = total.astype(BF)


def high_low(part):
    high = part.astype(BF)
    return high, (part - high.astype(F32)).astype(BF)


def back_body(ids, gradient, own, other, weight, partner, gain_parts, keep, extra, send, terms, parts, rows):
    c, xl, y = ids[1], ids[3], ids[4]
    mine = gradient[:, :, lanes(xl * 512, 512)].reshape(256, 512)
    theirs = gradient[:, :, lanes((1 - xl) * 512, 512)].reshape(256, 512)
    dims = (((1,), (1,)), ((), ()))
    for q in range(4):
        span = slice(q * 512, (q + 1) * 512)
        terms[:, span] = lax.dot_general(mine, weight[span, :], dims, preferred_element_type=F32) + lax.dot_general(
            theirs, partner[span, :], dims, preferred_element_type=F32
        )
    for m in range(2):
        for peer in range(NY):
            dy = (y + NY - peer) % NY
            place = (m * NY + peer) * 32
            encoder_rows = jnp.where(c == m, own[dy, 0].astype(F32), other[dy, 0].astype(F32))
            product = terms[place : place + 32, :] * encoder_rows
            if place == 0:
                parts[...] = jnp.sum(product, axis=0, keepdims=True)
            else:
                parts[...] += jnp.sum(product, axis=0, keepdims=True)
            rows[place : place + 32, :] = jnp.broadcast_to(jnp.sum(product, axis=1, keepdims=True), (32, 128))
    row_sums = jnp.transpose(rows[...])[0:1, :]
    for parity, is_send in ((c, False), (1 - c, True)):
        extras = []
        for i in range(2):
            layer_gain = gain_parts[2 * i + parity]
            extras += [layer_gain[:, :1024], layer_gain[:, 1024:]]
        extras.append(
            jnp.concatenate([parts[:, lanes((2 * i + parity) * 512, 512)] for i in range(2)], axis=1)
        )
        extras.append(jnp.concatenate([row_sums, jnp.zeros((1, 768), F32)], axis=1))
        extras.append(jnp.zeros((2, 1024), F32))
        block = jnp.concatenate(extras, axis=0)
        for i in range(2):
            part = terms[:, lanes((2 * i + parity) * 512, 512)]
            if is_send:
                send[:256, i * 512 : (i + 1) * 512] = part.astype(BF)
            else:
                keep[:, i * 512 : (i + 1) * 512] = part
        if is_send:
            send[256:, :] = jnp.concatenate(high_low(block), axis=0)
        else:
            extra[...] = block


def merge_body(ids, keep, extra, received, out):
    carried = received[256:, :].astype(F32)
    extras = extra[...] + carried[0:8] + carried[8:16]
    for xh in range(2):
        span = slice(xh * 512, (xh + 1) * 512)
        block = jnp.concatenate(
            [
                extras[2 * xh : 2 * xh + 1, :512],
                extras[2 * xh : 2 * xh + 1, 512:],
                extras[2 * xh + 1 : 2 * xh + 2, :512],
                extras[2 * xh + 1 : 2 * xh + 2, 512:],
                extras[4:5, span],
                extras[5:6, :512],
                jnp.zeros((2, 512), F32),
            ],
            axis=0,
        )
        block = jnp.concatenate(high_low(block), axis=0)
        for y in range(NY):
            for m in range(2):
                place = (m * NY + y) * 32
                part = keep[place : place + 32, span] + received[place : place + 32, span].astype(F32)
                out[xh * NY + y, m * 32 : (m + 1) * 32, :] = part.astype(BF)
            out[xh * NY + y, 64:, :] = block


def finish_body(ids, received, states, factor, final_gain, gradient, sums, rows):
    y = ids[4]
    total = received[0].astype(F32)
    for k in range(1, 8):
        total += received[k].astype(F32)
    extras = total[64:72] + total[72:80]
    sums[...] = extras
    rows[...] = jnp.transpose(jnp.broadcast_to(extras[5:6, :256], (128, 256)))
    for m in range(2):
        span = slice(m * 32, (m + 1) * 32)
        row_sum = rows[lanes(m * 128 + y * 32, 32), 0:1]
        scale = factor[span, 0:1]
        scaled = total[span] * final_gain[...].astype(F32)
        wide = states[span, :].astype(F32)
        gradient[span, :] = scale * scaled - wide * (scale * scale * (row_sum / D))


def touch_body(ids, after, block, out):
    pass


def touch(ids, block, after):
    return pl.pallas_call(
        touch_body,
        out_shape=jax.ShapeDtypeStruct(block.shape, block.dtype),
        in_specs=[pl.BlockSpec(memory_space=pltpu.SMEM)] + [pl.BlockSpec(memory_space=pl.ANY)] * 2,
        out_specs=pl.BlockSpec(memory_space=pl.ANY),
        input_output_aliases={2: 0},
    )(ids, after, block)


def per_device(
    encoder_states, encoder_lengths, final_gain, decoder_states, query_gain, cross_weight, upstream
):
    xh, c, z, xl, y = (lax.axis_index(axis) for axis in AXES)
    block = cross_weight[0].reshape(32, 8, 512).transpose(1, 0, 2)
    block = lax.all_to_all(block, ("xl", "y"), 0, 0, tiled=True).reshape(256, 512)
    weight = lax.all_gather(block, "z", axis=0, tiled=True)

    ids = jnp.stack([xh, c, z, xl, y, encoder_lengths[0, 0], encoder_lengths[1, 0], 0]).astype(jnp.int32)
    states = encoder_states.reshape(64, 512)
    stream = lax.dynamic_slice(decoder_states, (xh, c * ROWS, 0), (1, ROWS, D))[0]
    incoming = lax.dynamic_slice(upstream, (xh, c * ROWS, 0), (1, ROWS, D))[0]
    (pack,) = kernel_call(pack_body, ids, (states, final_gain[None], query_gain), [((80, 512), BF)])
    packs = [pack, shift(pack, core=1), shift(pack, xh=1), shift(pack, xh=1, core=1)]
    half, factor, query_gains = kernel_call(
        norm_body,
        ids,
        packs,
        [((32, D), BF), ((64, 128), F32), ((4, 1, D), F32)],
        [((64, D), F32), ((1, D), F32)],
    )
    both = jnp.stack([half, shift(half, xl=1)])
    own_rows = jnp.stack([both] + [shift(both, y=dy) for dy in range(1, NY)])
    other_rows = shift(own_rows, core=1)
    partner_block = shift(block, xl=1)

    (projected,) = kernel_call(
        project_body, ids, (own_rows, other_rows, weight), [((16, 32, 512), BF)], [((256, 512), BF)]
    )
    partner = lax.all_gather(touch(ids, partner_block, projected), "z", axis=0, tiled=True)
    own_pairs = lax.all_to_all(projected, ("xh", "xl", "y"), 0, 0, tiled=True)
    other_pairs = shift(own_pairs, core=1)
    keep, send, gain_parts = kernel_call(
        decoder_body,
        ids,
        (own_pairs, other_pairs, stream, incoming, query_gains),
        [((2, 32, 4096), BF), ((2, 32, 4096), BF), ((4, 1, D), F32)],
        [
            ((4, 32, 4096), BF),
            ((5, ROWS, D), BF),
            ((4, ROWS, D), BF),
            ((4, GROUPS, ENC, 128), F32),
            ((ROWS, D), F32),
            ((ROWS, D), F32),
            ((4, 32, 4096), BF),
        ],
    )
    (joined,) = kernel_call(join_body, ids, (keep, shift(send, core=1)), [((8, 32, 1024), BF)])
    joined = lax.all_to_all(joined, ("xh", "y"), 0, 0, tiled=True)
    term_keep, extra, term_send = kernel_call(
        back_body,
        ids,
        (joined, own_rows, other_rows, weight, partner, gain_parts),
        [((256, 1024), F32), ((8, 1024), F32), ((272, 1024), BF)],
        [((256, D), F32), ((1, D), F32), ((256, 128), F32)],
    )
    (merged,) = kernel_call(
        merge_body, ids, (term_keep, extra, shift(term_send, core=1)), [((8, 80, 512), BF)]
    )
    merged = lax.all_to_all(merged, ("xh", "y"), 0, 0, tiled=True)
    gradient, sums = kernel_call(
        finish_body,
        ids,
        (merged, states, factor, final_gain[None]),
        [((64, 512), F32), ((8, 512), F32)],
        [((256, 128), F32)],
    )
    for move in ({"xl": 1}, {"z": 1}, {"z": 2}, {"z": 4}):
        sums = sums + shift(sums, **move)
    final_gradient = sums[4] / final_gain.astype(F32)
    return (gradient.reshape(2, 32, 512), final_gradient, sums[:4].reshape(1, D))


def solution(mesh):
    dp, section = ("z", "xl", "y"), ("xh", "core")
    return jax.shard_map(
        per_device,
        mesh=Mesh(mesh.devices.reshape(SIZES), AXES),
        in_specs=(
            P(None, dp, section),
            P(None, dp),
            P(section),
            P(None, dp, None),
            P(section, None),
            P(section, dp, None),
            P(None, dp, None),
        ),
        out_specs=(P(None, dp, section), P(section), P(section, None)),
        check_vma=False,
    )
```

```python
import jax
import jax.numpy as jnp
import numpy as np
from jax import lax
from jax.experimental import pallas as pl
from jax.experimental.pallas import tpu as pltpu
from jax.sharding import Mesh
from jax.sharding import PartitionSpec as P

D = 2048
HEAD = 64
ENC = 32
ROWS = 32
LAYERS = 4
GROUPS = 8
EPSILON = 1e-06
AXES = ("xh", "core", "z", "xl", "y")
SIZES = (2, 2, 8, 2, 4)
NY = 4
BF, F32 = jnp.bfloat16, jnp.float32
MIB = 1 << 20


def shift(block, **moves):
    pairs = []
    for index in np.ndindex(*SIZES):
        to = list(index)
        for axis, by in moves.items():
            k = AXES.index(axis)
            to[k] = (index[k] + by) % SIZES[k] if axis in "yz" else index[k] ^ by
        pairs.append((int(np.ravel_multi_index(index, SIZES)), int(np.ravel_multi_index(to, SIZES))))
    return lax.ppermute(block, AXES, pairs)


def kernel_call(body, operands, outs, scratch=(), scalars=0, far=(), limit=16):
    spaces = [pltpu.SMEM if i < scalars else pl.ANY if i in far else pltpu.VMEM for i in range(len(operands))]
    return pl.pallas_call(
        body,
        out_shape=[jax.ShapeDtypeStruct(s, d) for s, d in outs],
        in_specs=[pl.BlockSpec(memory_space=space) for space in spaces],
        out_specs=[pl.BlockSpec(memory_space=pltpu.VMEM)] * len(outs),
        scratch_shapes=[x if hasattr(x, "dtype") and not isinstance(x, tuple) else pltpu.VMEM(*x) for x in scratch],
        compiler_params=pltpu.CompilerParams(vmem_limit_bytes=limit * MIB),
    )(*operands)


def coordinates(*axes):
    return tuple(lax.axis_index(axis) for axis in axes)


def lanes(start, size):
    return pl.ds(pl.multiple_of(start, size), size)


def pack_body(states, final_gain, query_gain, pack):
    pack[:64, :] = states[...]
    gains = [final_gain[...].astype(F32)]
    gains += [query_gain[:, i * 512 : (i + 1) * 512].astype(F32) for i in range(4)]
    gains += [jnp.zeros((11, 512), F32)]
    pack[64:, :] = jnp.concatenate(gains, axis=0).astype(BF)


def norm_body(p0, p1, p2, p3, half, factor, query_gains, wide, final_gains):
    xh, c = coordinates("xh", "core")
    section = xh * 2 + c
    for j, pack in enumerate((p0, p1, p2, p3)):
        peer = section ^ j
        wide[:, lanes(peer * 512, 512)] = pack[:64, :].astype(F32)
        gains = pack[64:, :].astype(F32)
        final_gains[:, lanes(peer * 512, 512)] = gains[0:1]
        for i in range(4):
            query_gains[peer, :, i * 512 : (i + 1) * 512] = gains[1 + i : 2 + i]
    states = wide[...]
    scale = lax.rsqrt(jnp.mean(states * states, axis=-1, keepdims=True) + EPSILON)
    factor[...] = jnp.broadcast_to(scale, (64, 128))
    wide[...] = states * scale * final_gains[...]
    half[...] = wide[lanes(c * 32, 32), :].astype(BF)


def project_body(own, other, weight, out, held, result):
    c, xl, y = coordinates("core", "xl", "y")
    for i, rows in enumerate((own, other)):
        m = (c + i) % 2
        result[...] = jnp.dot(rows[...].reshape(256, D), weight[...], preferred_element_type=F32).astype(BF)
        for dy in range(NY):
            for dxl in range(2):
                place = m * 8 + (xl + dxl) % 2 * 4 + (y + NY - dy) % NY
                k = dy * 2 + dxl
                if dxl == 0:
                    held[m, place % 4] = rows[dy, 0]
                out[place] = result[k * 32 : (k + 1) * 32, :]


def decoder_body(lengths, own, other, stream_in, upstream, query_gains, keep, send, gain_parts,
                 pairs, streams, queries, softmax, incoming, gradients):
    xh, c = coordinates("xh", "core")
    length = lengths[xh, 0]
    for i in range(2):
        for k in range(8):
            pairs[2 * i + c, :, k * 512 : (k + 1) * 512] = own[8 * i + k]
            pairs[2 * i + 1 - c, :, k * 512 : (k + 1) * 512] = other[8 * i + k]
    streams[0] = stream_in[...]
    incoming[...] = upstream[...].astype(F32)
    block = (lax.broadcasted_iota(jnp.int32, (128, 256), 0) // 32) == (
        lax.broadcasted_iota(jnp.int32, (128, 256), 1) // HEAD)
    block = jnp.where(block, 1.0, 0.0).astype(BF)
    lane = lax.broadcasted_iota(jnp.int32, (ROWS, 256), 1)
    visible = lax.broadcasted_iota(jnp.int32, (ENC, 1024), 0) < length
    scale = HEAD**-0.5
    def spread(part): return jnp.concatenate([part] * 4, axis=0) * block
    def fold(part):
        low = jnp.where(lane < 64, part[0:32], part[32:64])
        high = jnp.where(lane < 192, part[64:96], part[96:128])
        return jnp.where(lane < 128, low, high)
    def dot(a, b, dims): return lax.dot_general(a, b, (dims, ((), ())), preferred_element_type=F32)
    def col(g, base=0): return slice(base + g * 256, base + (g + 1) * 256)
    def lan(g): return slice(g * 128, (g + 1) * 128)
    G8 = range(GROUPS)
    def forward(layer, carry):
        wide = streams[layer].astype(F32)
        factor = lax.rsqrt(jnp.mean(wide * wide, axis=-1, keepdims=True) + EPSILON)
        q = (wide * factor * query_gains[layer]).astype(BF)
        queries[layer] = q
        scores = jnp.concatenate([dot(pairs[layer, :, col(g)], spread(q[:, col(g)]), ((1,), (1,))) for g in G8], axis=1) * scale
        scores = jnp.where(visible, scores, -1e30)
        highest = jnp.max(scores, axis=0, keepdims=True)
        weights = jnp.where(visible, jnp.exp(scores - highest), 0.0)
        rows = weights / jnp.sum(weights, axis=0, keepdims=True)
        softmax[layer] = rows
        narrow = rows.astype(BF)
        ctx = [fold(dot(narrow[:, lan(g)], pairs[layer, :, col(g, D)], ((0,), (0,)))) for g in G8]
        streams[layer + 1] = (wide + jnp.concatenate(ctx, axis=1)).astype(BF)
        return carry
    lax.fori_loop(0, LAYERS, forward, 0)
    def backward(turn, carry):
        layer = LAYERS - 1 - turn
        wide = streams[layer].astype(F32)
        factor = lax.rsqrt(jnp.mean(wide * wide, axis=-1, keepdims=True) + EPSILON)
        grad = incoming[...]
        narrow_grad = grad.astype(BF)
        rows = softmax[layer]
        narrow = rows.astype(BF)
        parts = []
        for g in G8:
            heads = spread(narrow_grad[:, col(g)])
            parts.append(dot(pairs[layer, :, col(g, D)], heads, ((1,), (1,))))
            gradients[layer, :, col(g, D)] = dot(narrow[:, lan(g)], heads, ((1,), (0,))).astype(BF)
        softmax_gradient = jnp.concatenate(parts, axis=1)
        ds = rows * (softmax_gradient - jnp.sum(rows * softmax_gradient, axis=0, keepdims=True))
        ds = ds.astype(BF)
        q = queries[layer]
        dq = []
        for g in G8:
            dq.append(fold(dot(ds[:, lan(g)], pairs[layer, :, col(g)], ((0,), (0,)))))
            gradients[layer, :, col(g)] = (dot(ds[:, lan(g)], spread(q[:, col(g)]), ((1,), (0,))) * scale).astype(BF)
        gradient = jnp.concatenate(dq, axis=1) * scale
        scaled = gradient * query_gains[layer]
        mean = jnp.mean(scaled * wide, axis=-1, keepdims=True)
        incoming[...] = grad + factor * scaled - wide * (factor * factor * factor) * mean
        gain_parts[layer] = jnp.sum(gradient * wide * factor, axis=0, keepdims=True)
        return carry
    lax.fori_loop(0, LAYERS, backward, 0)
    for i in range(2):
        keep[i] = gradients[2 * i + c]
        send[i] = gradients[2 * i + 1 - c]


def join_body(keep, received, out):
    for xh in range(2):
        for y in range(NY):
            for half in range(2):
                span = slice(half * 2048 + y * 512, half * 2048 + (y + 1) * 512)
                total = keep[xh, :, span].astype(F32) + received[xh, :, span].astype(F32)
                out[xh * NY + y, :, half * 512 : (half + 1) * 512] = total.astype(BF)


def high_low(part):
    high = part.astype(BF)
    return high, (part - high.astype(F32)).astype(BF)


def back_body(gradient, held, weight, partner, gain_parts, keep, extra, send, terms, parts, rows):
    c, xl = coordinates("core", "xl")
    mine = gradient[:, :, lanes(xl * 512, 512)].reshape(256, 512)
    theirs = gradient[:, :, lanes((1 - xl) * 512, 512)].reshape(256, 512)
    dims = (((1,), (1,)), ((), ()))
    for q in range(4):
        span = slice(q * 512, (q + 1) * 512)
        terms[:, span] = lax.dot_general(mine, weight[span, :], dims, preferred_element_type=F32) + lax.dot_general(
            theirs, partner[span, :], dims, preferred_element_type=F32
        )
    for m in range(2):
        for peer in range(NY):
            place = (m * NY + peer) * 32
            product = terms[place : place + 32, :] * held[m, peer].astype(F32)
            if place == 0:
                parts[...] = jnp.sum(product, axis=0, keepdims=True)
            else:
                parts[...] += jnp.sum(product, axis=0, keepdims=True)
            rows[place : place + 32, :] = jnp.broadcast_to(jnp.sum(product, axis=1, keepdims=True), (32, 128))
    row_sums = jnp.transpose(rows[...])[0:1, :]
    for parity, is_send in ((c, False), (1 - c, True)):
        extras = []
        for i in range(2):
            layer_gain = gain_parts[2 * i + parity]
            extras += [layer_gain[:, :1024], layer_gain[:, 1024:]]
        extras.append(
            jnp.concatenate([parts[:, lanes((2 * i + parity) * 512, 512)] for i in range(2)], axis=1)
        )
        extras.append(jnp.concatenate([row_sums, jnp.zeros((1, 768), F32)], axis=1))
        extras.append(jnp.zeros((2, 1024), F32))
        block = jnp.concatenate(extras, axis=0)
        for i in range(2):
            part = terms[:, lanes((2 * i + parity) * 512, 512)]
            if is_send:
                send[:256, i * 512 : (i + 1) * 512] = part.astype(BF)
            else:
                keep[:, i * 512 : (i + 1) * 512] = part
        if is_send:
            send[256:, :] = jnp.concatenate(high_low(block), axis=0)
        else:
            extra[...] = block


def merge_body(keep, extra, received, out):
    carried = received[256:, :].astype(F32)
    extras = extra[...] + carried[0:8] + carried[8:16]
    for xh in range(2):
        span = slice(xh * 512, (xh + 1) * 512)
        block = jnp.concatenate(
            [
                extras[2 * xh : 2 * xh + 1, :512],
                extras[2 * xh : 2 * xh + 1, 512:],
                extras[2 * xh + 1 : 2 * xh + 2, :512],
                extras[2 * xh + 1 : 2 * xh + 2, 512:],
                extras[4:5, span],
                extras[5:6, :512],
                jnp.zeros((2, 512), F32),
            ],
            axis=0,
        )
        block = jnp.concatenate(high_low(block), axis=0)
        for y in range(NY):
            for m in range(2):
                place = (m * NY + y) * 32
                part = keep[place : place + 32, span] + received[place : place + 32, span].astype(F32)
                out[xh * NY + y, m * 32 : (m + 1) * 32, :] = part.astype(BF)
            out[xh * NY + y, 64:, :] = block


def finish_body(received, states, factor, final_gain, gradient, sums, rows):
    (y,) = coordinates("y")
    total = received[0].astype(F32)
    for k in range(1, 8):
        total += received[k].astype(F32)
    extras = total[64:72] + total[72:80]
    sums[...] = extras
    rows[...] = jnp.transpose(jnp.broadcast_to(extras[5:6, :256], (128, 256)))
    for m in range(2):
        span = slice(m * 32, (m + 1) * 32)
        row_sum = rows[lanes(m * 128 + y * 32, 32), 0:1]
        scale = factor[span, 0:1]
        scaled = total[span] * final_gain[...].astype(F32)
        wide = states[span, :].astype(F32)
        gradient[span, :] = scale * scaled - wide * (scale * scale * (row_sum / D))


def per_device(
    encoder_states, encoder_lengths, final_gain, decoder_states, query_gain, cross_weight, upstream
):
    xh, c = coordinates("xh", "core")
    block = cross_weight[0].reshape(32, 8, 512).transpose(1, 0, 2)
    block = lax.all_to_all(block, ("xl", "y"), 0, 0, tiled=True).reshape(256, 512)
    weight = lax.all_gather(block, "z", axis=0, tiled=True)

    states = encoder_states.reshape(64, 512)
    stream = lax.dynamic_slice(decoder_states, (xh, c * ROWS, 0), (1, ROWS, D))[0]
    incoming = lax.dynamic_slice(upstream, (xh, c * ROWS, 0), (1, ROWS, D))[0]
    (pack,) = kernel_call(pack_body, (states, final_gain[None], query_gain), [((80, 512), BF)])
    packs = [pack, shift(pack, core=1), shift(pack, xh=1), shift(pack, xh=1, core=1)]
    half, factor, query_gains = kernel_call(
        norm_body,
        packs,
        [((32, D), BF), ((64, 128), F32), ((4, 1, D), F32)],
        [((64, D), F32), ((1, D), F32)],
    )
    both = jnp.stack([half, shift(half, xl=1)])
    own_rows = jnp.stack([both] + [shift(both, y=dy) for dy in range(1, NY)])
    other_rows = shift(own_rows, core=1)
    partner_block = shift(block, xl=1)

    projected, held = kernel_call(
        project_body,
        (own_rows, other_rows, weight),
        [((16, 32, 512), BF), ((2, NY, 32, D), BF)],
        [((256, 512), BF)],
    )
    partner = lax.all_gather(partner_block, "z", axis=0, tiled=True)
    own_pairs = lax.all_to_all(projected, ("xh", "xl", "y"), 0, 0, tiled=True)
    other_pairs = shift(own_pairs, core=1)
    keep, send, gain_parts = kernel_call(
        decoder_body,
        (encoder_lengths, own_pairs, other_pairs, stream, incoming, query_gains),
        [((2, 32, 4096), BF), ((2, 32, 4096), BF), ((4, 1, D), F32)],
        [
            ((4, 32, 4096), BF),
            ((5, ROWS, D), BF),
            ((4, ROWS, D), BF),
            ((4, ENC, 1024), F32),
            ((ROWS, D), F32),
            ((4, 32, 4096), BF),
        ],
        scalars=1,
    )
    (joined,) = kernel_call(join_body, (keep, shift(send, core=1)), [((8, 32, 1024), BF)])
    joined = lax.all_to_all(joined, ("xh", "y"), 0, 0, tiled=True)
    term_keep, extra, term_send = kernel_call(
        back_body,
        (joined, held, weight, partner, gain_parts),
        [((256, 1024), F32), ((8, 1024), F32), ((272, 1024), BF)],
        [((256, D), F32), ((1, D), F32), ((256, 128), F32)],
    )
    (merged,) = kernel_call(
        merge_body, (term_keep, extra, shift(term_send, core=1)), [((8, 80, 512), BF)]
    )
    merged = lax.all_to_all(merged, ("xh", "y"), 0, 0, tiled=True)
    gradient, sums = kernel_call(
        finish_body,
        (merged, states, factor, final_gain[None]),
        [((64, 512), F32), ((8, 512), F32)],
        [((256, 128), F32)],
    )
    sums = sums + shift(sums, xl=1)
    ahead = shift(sums, z=1)
    pair = sums + ahead
    triple = pair + shift(sums, z=-1)
    sums = triple + shift(triple, z=-3) + shift(pair, z=2)
    final_gradient = sums[4] / final_gain.astype(F32)
    return (gradient.reshape(2, 32, 512), final_gradient, sums[:4].reshape(1, D))


def solution(mesh):
    dp, section = ("z", "xl", "y"), ("xh", "core")
    return jax.shard_map(
        per_device,
        mesh=Mesh(mesh.devices.reshape(SIZES), AXES),
        in_specs=(
            P(None, dp, section),
            P(None, dp),
            P(section),
            P(None, dp, None),
            P(section, None),
            P(section, dp, None),
            P(None, dp, None),
        ),
        out_specs=(P(None, dp, section), P(section), P(section, None)),
        check_vma=False,
    )
```

```python
import jax
import jax.numpy as jnp
import numpy as np
from jax import lax
from jax.experimental import pallas as pl
from jax.experimental.pallas import tpu as pltpu
from jax.sharding import Mesh
from jax.sharding import PartitionSpec as P

D = 2048
HEAD = 64
ENC = 32
ROWS = 32
LAYERS = 4
GROUPS = 8
EPSILON = 1e-06
AXES = ("xh", "core", "z", "xl", "y")
SIZES = (2, 2, 8, 2, 4)
NY = 4
BF, F32 = jnp.bfloat16, jnp.float32
MIB = 1 << 20


def shift(block, **moves):
    pairs = []
    for index in np.ndindex(*SIZES):
        to = list(index)
        for axis, by in moves.items():
            k = AXES.index(axis)
            to[k] = (index[k] + by) % SIZES[k] if axis in "yz" else index[k] ^ by
        pairs.append((int(np.ravel_multi_index(index, SIZES)), int(np.ravel_multi_index(to, SIZES))))
    return lax.ppermute(block, AXES, pairs)


def kernel_call(body, operands, outs, scratch=(), scalars=0, far=(), far_outs=(), aliases=None, limit=16):
    operands = [
        pltpu.with_memory_space_constraint(x, pltpu.HBM) if i in far else x for i, x in enumerate(operands)
    ]
    spaces = [pltpu.SMEM if i < scalars else pltpu.HBM if i in far else pltpu.VMEM for i in range(len(operands))]
    return pl.pallas_call(
        body,
        out_shape=[
            pltpu.HBM(s, d) if i in far_outs else jax.ShapeDtypeStruct(s, d) for i, (s, d) in enumerate(outs)
        ],
        in_specs=[pl.BlockSpec(memory_space=space) for space in spaces],
        out_specs=[pl.BlockSpec(memory_space=pltpu.HBM if i in far_outs else pltpu.VMEM) for i in range(len(outs))],
        scratch_shapes=[pltpu.VMEM(*x) if isinstance(x, tuple) else x for x in scratch],
        input_output_aliases=aliases or {},
        compiler_params=pltpu.CompilerParams(vmem_limit_bytes=limit * MIB),
    )(*operands)


def coordinates(*axes):
    return tuple(lax.axis_index(axis) for axis in axes)


def lanes(start, size):
    return pl.ds(pl.multiple_of(start, size), size)


RING = (0, -1, 1, -2, 2, -3, 3, -4, -4)


def pack_body(states, final_gain, query_gain, pack):
    pack[:64, :] = states[...]
    gains = [final_gain[...].astype(F32)]
    gains += [query_gain[:, i * 512 : (i + 1) * 512].astype(F32) for i in range(4)]
    gains += [jnp.zeros((11, 512), F32)]
    pack[64:, :] = jnp.concatenate(gains, axis=0).astype(BF)


def norm_body(p0, p1, p2, p3, ahead_in, behind_in, streams, upstreams,
              half, factor, query_gains, stream, upstream, ahead, behind, wide, final_gains, sems):
    xh, c = coordinates("xh", "core")
    mine = pl.ds(pl.multiple_of(c * ROWS, ROWS), ROWS)
    copies = [
        pltpu.make_async_copy(streams.at[xh, mine], stream, sems.at[0]),
        pltpu.make_async_copy(upstreams.at[xh, mine], upstream, sems.at[1]),
    ]
    for copy in copies:
        copy.start()
    section = xh * 2 + c
    for j, pack in enumerate((p0, p1, p2, p3)):
        peer = section ^ j
        wide[:, lanes(peer * 512, 512)] = pack[:64, :].astype(F32)
        gains = pack[64:, :].astype(F32)
        final_gains[:, lanes(peer * 512, 512)] = gains[0:1]
        for i in range(4):
            query_gains[peer, :, i * 512 : (i + 1) * 512] = gains[1 + i : 2 + i]
    states = wide[...]
    scale = lax.rsqrt(jnp.mean(states * states, axis=-1, keepdims=True) + EPSILON)
    factor[...] = jnp.broadcast_to(scale, (64, 128))
    wide[...] = states * scale * final_gains[...]
    half[...] = wide[lanes(c * 32, 32), :].astype(BF)
    for copy in copies:
        copy.wait()


def near_body(half, p1, p2, p3, across_in, ahead_in, behind_in, near, others, across, ahead, behind):
    near[0] = half[...]
    for k, part in enumerate((p1, p2, p3)):
        near[k + 1] = part[...]
        others[k] = part[...]


def group_body(near, across, beyond, ahead_in, behind_in, rows, upper, lower, ahead, behind):
    rows[0, 1] = across[...]
    for k in range(NY):
        rows[k, 0] = near[k]
        if k:
            rows[k, 1] = beyond[k - 1]
    upper[...] = ahead_in[:128]
    lower[...] = behind_in[128:]


def project_body(own, other, *refs):
    blocks, (out, held, weight_out, weight, result, sems) = refs[:9], refs[9:]
    c, z, xl, y = coordinates("core", "z", "xl", "y")
    copies = []
    for i, rows in enumerate((own, other)):
        for dy in range(NY):
            for dxl in range(2):
                place = held.at[(c + i) % 2, (xl + dxl) % 2 * 4 + (y + NY - dy) % NY]
                copies.append(pltpu.make_async_copy(rows.at[dy, dxl], place, sems.at[i * 8 + dy * 2 + dxl]))
                copies[-1].start()
    for k, block in enumerate(blocks):
        place = (z + 8 + RING[k]) % 8 * 256 + 128 * (k == 8)
        weight[pl.ds(pl.multiple_of(place, 128), block.shape[0]), :] = block[...]
    copies.append(pltpu.make_async_copy(weight, weight_out, sems.at[16]))
    copies[-1].start()
    for i, rows in enumerate((own, other)):
        result[...] = jnp.dot(rows[...].reshape(256, D), weight[...], preferred_element_type=F32).astype(BF)
        for dy in range(NY):
            for dxl in range(2):
                place = (c + i) % 2 * 8 + (xl + dxl) % 2 * 4 + (y + NY - dy) % NY
                row = (dy * 2 + dxl) * 32
                out[place] = result[row : row + 32, :]
    for copy in copies:
        copy.wait()


def decoder_body(lengths, own, other, stream_in, upstream, query_gains, keep, send, gain_parts,
                 pairs, streams, queries, softmax, incoming, gradients):
    xh, c = coordinates("xh", "core")
    for i in range(2):
        pairs[2 * i + c] = own[8 * i : 8 * i + 8]
        pairs[2 * i + 1 - c] = other[8 * i : 8 * i + 8]
    streams[0] = stream_in[...]
    incoming[...] = upstream[...].astype(F32)
    length = lengths[xh, 0]
    block = (lax.broadcasted_iota(jnp.int32, (128, 256), 0) // 32) == (
        lax.broadcasted_iota(jnp.int32, (128, 256), 1) // HEAD)
    block = jnp.where(block, 1.0, 0.0).astype(BF)
    lane = lax.broadcasted_iota(jnp.int32, (ROWS, 256), 1)
    visible = lax.broadcasted_iota(jnp.int32, (ENC, 1024), 0) < length
    scale = HEAD**-0.5
    def spread(part):
        return jnp.concatenate([part] * 4, axis=0) * block
    def fold(part):
        low = jnp.where(lane < 64, part[0:32], part[32:64])
        high = jnp.where(lane < 192, part[64:96], part[96:128])
        return jnp.where(lane < 128, low, high)
    def dot(a, b, dims):
        return lax.dot_general(a, b, (dims, ((), ())), preferred_element_type=F32)
    def col(g, base=0):
        return slice(base + g * 256, base + (g + 1) * 256)

    def lan(g):
        return slice(g * 128, (g + 1) * 128)

    def keys(layer, g):
        return pairs[layer, g // 2, :, col(g % 2)]

    def values(layer, g):
        return pairs[layer, 4 + g // 2, :, col(g % 2)]

    for layer in range(LAYERS):
        wide = streams[layer].astype(F32)
        factor = lax.rsqrt(jnp.mean(wide * wide, axis=-1, keepdims=True) + EPSILON)
        q = (wide * factor * query_gains[layer]).astype(BF)
        queries[layer] = q
        scores = jnp.concatenate([dot(keys(layer, g), spread(q[:, col(g)]), ((1,), (1,))) for g in range(GROUPS)], axis=1) * scale
        scores = jnp.where(visible, scores, -1e30)
        highest = jnp.max(scores, axis=0, keepdims=True)
        weights = jnp.where(visible, jnp.exp(scores - highest), 0.0)
        rows = weights / jnp.sum(weights, axis=0, keepdims=True)
        softmax[layer] = rows
        narrow = rows.astype(BF)
        ctx = [fold(dot(narrow[:, lan(g)], values(layer, g), ((0,), (0,)))) for g in range(GROUPS)]
        streams[layer + 1] = (wide + jnp.concatenate(ctx, axis=1)).astype(BF)
    for layer in reversed(range(LAYERS)):
        wide = streams[layer].astype(F32)
        factor = lax.rsqrt(jnp.mean(wide * wide, axis=-1, keepdims=True) + EPSILON)
        grad = incoming[...]
        narrow_grad = grad.astype(BF)
        rows = softmax[layer]
        narrow = rows.astype(BF)
        parts = []
        for g in range(GROUPS):
            heads = spread(narrow_grad[:, col(g)])
            parts.append(dot(values(layer, g), heads, ((1,), (1,))))
            gradients[layer, :, col(g, D)] = dot(narrow[:, lan(g)], heads, ((1,), (0,))).astype(BF)
        softmax_gradient = jnp.concatenate(parts, axis=1)
        ds = rows * (softmax_gradient - jnp.sum(rows * softmax_gradient, axis=0, keepdims=True))
        ds = ds.astype(BF)
        q = queries[layer]
        dq = []
        for g in range(GROUPS):
            dq.append(fold(dot(ds[:, lan(g)], keys(layer, g), ((0,), (0,)))))
            gradients[layer, :, col(g)] = (dot(ds[:, lan(g)], spread(q[:, col(g)]), ((1,), (0,))) * scale).astype(BF)
        gradient = jnp.concatenate(dq, axis=1) * scale
        scaled = gradient * query_gains[layer]
        mean = jnp.mean(scaled * wide, axis=-1, keepdims=True)
        incoming[...] = grad + factor * scaled - wide * (factor * factor * factor) * mean
        gain_parts[layer] = jnp.sum(gradient * wide * factor, axis=0, keepdims=True)
    for i in range(2):
        keep[i] = gradients[2 * i + c]
        send[i] = gradients[2 * i + 1 - c]


def join_body(keep, received, out):
    for xh in range(2):
        for k in range(8):
            span = slice(k * 512, (k + 1) * 512)
            total = keep[xh, :, span].astype(F32) + received[xh, :, span].astype(F32)
            out[xh * 8 + k] = total.astype(BF)


def high_low(part):
    high = part.astype(BF)
    return high, (part - high.astype(F32)).astype(BF)


def back_body(gradient, held_far, weight, gain_parts, keep, extra, send, terms, parts, rows, held, sem):
    (c,) = coordinates("core")
    copy = pltpu.make_async_copy(held_far, held, sem)
    copy.start()
    flat = gradient[...].reshape(512, 512)
    for q in range(4):
        span = slice(q * 512, (q + 1) * 512)
        terms[:, span] = lax.dot_general(flat, weight[span, :], (((1,), (1,)), ((), ())), preferred_element_type=F32)
    copy.wait()
    for m in range(2):
        for peer in range(8):
            place = (m * 8 + peer) * 32
            product = terms[place : place + 32, :] * held[m, peer].astype(F32)
            if place == 0:
                parts[...] = jnp.sum(product, axis=0, keepdims=True)
            else:
                parts[...] += jnp.sum(product, axis=0, keepdims=True)
            rows[place : place + 32, :] = jnp.broadcast_to(jnp.sum(product, axis=1, keepdims=True), (32, 128))
    row_sums = jnp.transpose(rows[...])[0:1, :]
    for parity, is_send in ((c, False), (1 - c, True)):
        extras = []
        for i in range(2):
            layer_gain = gain_parts[2 * i + parity]
            extras += [layer_gain[:, :1024], layer_gain[:, 1024:]]
        extras.append(
            jnp.concatenate([parts[:, lanes((2 * i + parity) * 512, 512)] for i in range(2)], axis=1)
        )
        extras.append(jnp.concatenate([row_sums, jnp.zeros((1, 512), F32)], axis=1))
        extras.append(jnp.zeros((2, 1024), F32))
        block = jnp.concatenate(extras, axis=0)
        for i in range(2):
            part = terms[:, lanes((2 * i + parity) * 512, 512)]
            if is_send:
                send[:512, i * 512 : (i + 1) * 512] = part.astype(BF)
            else:
                keep[:, i * 512 : (i + 1) * 512] = part
        if is_send:
            send[512:, :] = jnp.concatenate(high_low(block), axis=0)
        else:
            extra[...] = block


def merge_body(keep, extra, received, out):
    carried = received[512:, :].astype(F32)
    extras = extra[...] + carried[0:8] + carried[8:16]
    for xh in range(2):
        span = slice(xh * 512, (xh + 1) * 512)
        block = jnp.concatenate(
            [
                extras[2 * xh : 2 * xh + 1, :512],
                extras[2 * xh : 2 * xh + 1, 512:],
                extras[2 * xh + 1 : 2 * xh + 2, :512],
                extras[2 * xh + 1 : 2 * xh + 2, 512:],
                extras[4:5, span],
                extras[5:6, :512],
                jnp.zeros((2, 512), F32),
            ],
            axis=0,
        )
        block = jnp.concatenate(high_low(block), axis=0)
        for k in range(8):
            for m in range(2):
                place = (m * 8 + k) * 32
                part = keep[place : place + 32, span] + received[place : place + 32, span].astype(F32)
                out[xh * 8 + k, m * 32 : (m + 1) * 32, :] = part.astype(BF)
            out[xh * 8 + k, 64:, :] = block


def finish_body(received, states, factor, final_gain, gradient, sums, rows):
    xl, y = coordinates("xl", "y")
    total = received[0].astype(F32)
    for k in range(1, 16):
        total += received[k].astype(F32)
    extras = total[64:72] + total[72:80]
    sums[...] = extras
    rows[...] = jnp.transpose(jnp.broadcast_to(extras[5:6], (128, 512)))
    for m in range(2):
        span = slice(m * 32, (m + 1) * 32)
        row_sum = rows[lanes(m * 256 + (xl * 4 + y) * 32, 32), 0:1]
        scale = factor[span, 0:1]
        scaled = total[span] * final_gain[...].astype(F32)
        wide = states[span, :].astype(F32)
        gradient[span, :] = scale * scaled - wide * (scale * scale * (row_sum / D))


def close_body(first, second, third, final_gain, final_gradient, layers_gradient):
    total = first[...] + second[...] + third[...]
    for i in range(4):
        layers_gradient[:, i * 512 : (i + 1) * 512] = total[i : i + 1]
    final_gradient[...] = total[4:5] / final_gain[...].astype(F32)


def per_device(
    encoder_states, encoder_lengths, final_gain, decoder_states, query_gain, cross_weight, upstream
):
    block = lax.all_to_all(cross_weight[0], ("xl", "y"), 1, 0, tiled=True)
    states = encoder_states.reshape(64, 512)
    (pack,) = kernel_call(pack_body, (states, final_gain[None], query_gain), [((80, 512), BF)])
    packs = [pack, shift(pack, core=1), shift(pack, xh=1), shift(pack, xh=1, core=1)]
    tile = ((256, 512), BF)
    half, factor, query_gains, stream, incoming, ahead1, behind1 = kernel_call(
        norm_body,
        packs + [shift(block, z=1), shift(block, z=-1), decoder_states, upstream],
        [((32, D), BF), ((64, 128), F32), ((4, 1, D), F32), ((ROWS, D), BF), ((ROWS, D), BF), tile, tile],
        [((64, D), F32), ((1, D), F32), pltpu.SemaphoreType.DMA((2,))],
        far=(6, 7),
        aliases={4: 5, 5: 6},
    )
    near, others, across, ahead2, behind2 = kernel_call(
        near_body,
        [half] + [shift(half, y=dy) for dy in range(1, NY)]
        + [shift(half, xl=1), shift(ahead1, z=1), shift(behind1, z=-1)],
        [((NY, 32, D), BF), ((NY - 1, 32, D), BF), ((32, D), BF), tile, tile],
        aliases={4: 2, 5: 3, 6: 4},
    )
    own_rows, upper, lower, ahead3, behind3 = kernel_call(
        group_body,
        [near, across, shift(others, xl=1), shift(ahead2, z=1), shift(behind2, z=-1)],
        [((NY, 2, 32, D), BF), ((128, 512), BF), ((128, 512), BF), tile, tile],
        aliases={3: 3, 4: 4},
    )
    ring = [block, ahead1, behind1, ahead2, behind2, ahead3, behind3, shift(upper, z=1), shift(lower, z=-1)]
    projected, held, weight = kernel_call(
        project_body,
        [own_rows, shift(own_rows, core=1)] + ring,
        [((16, 32, 512), BF), ((2, 8, 32, D), BF), ((D, 512), BF)],
        [((D, 512), BF), ((256, 512), BF), pltpu.SemaphoreType.DMA((17,))],
        far_outs=(1, 2),
    )
    own_pairs = lax.all_to_all(projected, ("xh", "xl", "y"), 0, 0, tiled=True)
    other_pairs = shift(own_pairs, core=1)
    keep, send, gain_parts = kernel_call(
        decoder_body,
        (encoder_lengths, own_pairs, other_pairs, stream, incoming, query_gains),
        [((2, 32, 4096), BF), ((2, 32, 4096), BF), ((4, 1, D), F32)],
        [
            ((4, 8, 32, 512), BF),
            ((5, ROWS, D), BF),
            ((4, ROWS, D), BF),
            ((4, ENC, 1024), F32),
            ((ROWS, D), F32),
            ((4, 32, 4096), BF),
        ],
        scalars=1,
    )
    (joined,) = kernel_call(join_body, (keep, shift(send, core=1)), [((16, 32, 512), BF)])
    joined = lax.all_to_all(joined, ("xh", "xl", "y"), 0, 0, tiled=True)
    term_keep, extra, term_send = kernel_call(
        back_body,
        (joined, held, weight, gain_parts),
        [((512, 1024), F32), ((8, 1024), F32), ((528, 1024), BF)],
        [
            ((512, D), F32),
            ((1, D), F32),
            ((512, 128), F32),
            ((2, 8, 32, D), BF),
            pltpu.SemaphoreType.DMA,
        ],
        far=(1,),
    )
    (merged,) = kernel_call(
        merge_body, (term_keep, extra, shift(term_send, core=1)), [((16, 80, 512), BF)]
    )
    merged = lax.all_to_all(merged, ("xh", "xl", "y"), 0, 0, tiled=True)
    gradient, sums = kernel_call(
        finish_body,
        (merged, states, factor, final_gain[None]),
        [((64, 512), F32), ((8, 512), F32)],
        [((512, 128), F32)],
    )
    ahead = shift(sums, z=1)
    pair = sums + ahead
    triple = pair + shift(sums, z=-1)
    final_gradient, layers_gradient = kernel_call(
        close_body,
        (triple, shift(triple, z=-3), shift(pair, z=2), final_gain[None]),
        [((1, 512), F32), ((1, D), F32)],
    )
    return (gradient.reshape(2, 32, 512), final_gradient[0], layers_gradient)


def solution(mesh):
    dp, section = ("z", "xl", "y"), ("xh", "core")
    return jax.shard_map(
        per_device,
        mesh=Mesh(mesh.devices.reshape(SIZES), AXES),
        in_specs=(
            P(None, dp, section),
            P(None, dp),
            P(section),
            P(None, dp, None),
            P(section, None),
            P(section, dp, None),
            P(None, dp, None),
        ),
        out_specs=(P(None, dp, section), P(section), P(section, None)),
        check_vma=False,
    )
```

```python
import jax
import jax.numpy as jnp
import numpy as np
from jax import lax
from jax.experimental import pallas as pl
from jax.experimental.pallas import tpu as pltpu
from jax.sharding import Mesh
from jax.sharding import PartitionSpec as P

D = 2048
HEAD = 64
ENC = 32
ROWS = 32
LAYERS = 4
GROUPS = 8
EPSILON = 1e-06
AXES = ("xh", "core", "z", "xl", "y")
SIZES = (2, 2, 8, 2, 4)
NY = 4
BF, F32 = jnp.bfloat16, jnp.float32
MIB = 1 << 20


def shift(block, **moves):
    pairs = []
    for index in np.ndindex(*SIZES):
        to = list(index)
        for axis, by in moves.items():
            k = AXES.index(axis)
            to[k] = (index[k] + by) % SIZES[k] if axis in "yz" else index[k] ^ by
        pairs.append((int(np.ravel_multi_index(index, SIZES)), int(np.ravel_multi_index(to, SIZES))))
    return lax.ppermute(block, AXES, pairs)


def kernel_call(body, operands, outs, scratch=(), scalars=0, far=(), far_outs=(), near_outs=(), aliases=None, limit=16):
    operands = [
        pltpu.with_memory_space_constraint(x, pltpu.HBM) if i in far else x for i, x in enumerate(operands)
    ]
    spaces = [pltpu.SMEM if i < scalars else pltpu.HBM if i in far else pltpu.VMEM for i in range(len(operands))]
    return pl.pallas_call(
        body,
        out_shape=[
            pltpu.HBM(s, d) if i in far_outs else pltpu.VMEM(s, d) if i in near_outs else jax.ShapeDtypeStruct(s, d)
            for i, (s, d) in enumerate(outs)
        ],
        in_specs=[pl.BlockSpec(memory_space=space) for space in spaces],
        out_specs=[pl.BlockSpec(memory_space=pltpu.HBM if i in far_outs else pltpu.VMEM) for i in range(len(outs))],
        scratch_shapes=[pltpu.VMEM(*x) if isinstance(x, tuple) else x for x in scratch],
        input_output_aliases=aliases or {},
        compiler_params=pltpu.CompilerParams(vmem_limit_bytes=limit * MIB),
    )(*operands)


def coordinates(*axes):
    return tuple(lax.axis_index(axis) for axis in axes)


def lanes(start, size):
    return pl.ds(pl.multiple_of(start, size), size)


RING = (0, -1, 1, -2, 2, -3, 3, -4, -4)


def pack_body(weight, states, final_gain, query_gain, columns, pack, gain_row, gain, query, sems):
    copies = [
        pltpu.make_async_copy(states, pack.at[pl.ds(0, 64)], sems.at[8]),
        pltpu.make_async_copy(final_gain, gain, sems.at[9]),
        pltpu.make_async_copy(query_gain, query, sems.at[10]),
    ]
    for k in range(8):
        part = weight.at[0, :, pl.ds(k * 512, 512)]
        copies.append(pltpu.make_async_copy(part, columns.at[k], sems.at[k]))
    for copy in copies:
        copy.start()
    copies[1].wait()
    copies[2].wait()
    gain_row[...] = gain[...].astype(F32).reshape(1, 512)
    gains = [gain_row[...]]
    gains += [query[:, i * 512 : (i + 1) * 512].astype(F32) for i in range(4)]
    gains += [jnp.zeros((11, 512), F32)]
    pack[64:, :] = jnp.concatenate(gains, axis=0).astype(BF)
    copies[0].wait()
    for copy in copies[3:]:
        copy.wait()


def norm_body(p0, p1, p2, p3, ahead_in, behind_in, streams, upstreams,
              half, factor, query_gains, stream, upstream, ahead, behind, wide, final_gains, sems):
    xh, c = coordinates("xh", "core")
    mine = pl.ds(pl.multiple_of(c * ROWS, ROWS), ROWS)
    copies = [
        pltpu.make_async_copy(streams.at[xh, mine], stream, sems.at[0]),
        pltpu.make_async_copy(upstreams.at[xh, mine], upstream, sems.at[1]),
    ]
    for copy in copies:
        copy.start()
    section = xh * 2 + c
    for j, pack in enumerate((p0, p1, p2, p3)):
        peer = section ^ j
        wide[:, lanes(peer * 512, 512)] = pack[:64, :].astype(F32)
        gains = pack[64:, :].astype(F32)
        final_gains[:, lanes(peer * 512, 512)] = gains[0:1]
        for i in range(4):
            query_gains[peer, :, i * 512 : (i + 1) * 512] = gains[1 + i : 2 + i]
    states = wide[...]
    scale = lax.rsqrt(jnp.mean(states * states, axis=-1, keepdims=True) + EPSILON)
    factor[...] = jnp.broadcast_to(scale, (64, 128))
    wide[...] = states * scale * final_gains[...]
    half[...] = wide[lanes(c * 32, 32), :].astype(BF)
    for copy in copies:
        copy.wait()


def near_body(across_in, half, p1, p2, p3, ahead_in, behind_in, near, others, across, ahead, behind):
    near[0] = half[...]
    for k, part in enumerate((p1, p2, p3)):
        near[k + 1] = part[...]
        others[k] = part[...]


def group_body(near, across, beyond, ahead_in, behind_in, rows, upper, lower, ahead, behind):
    rows[0, 1] = across[...]
    for k in range(NY):
        rows[k, 0] = near[k]
        if k:
            rows[k, 1] = beyond[k - 1]
    upper[...] = ahead_in[:128]
    lower[...] = behind_in[128:]


def own_places(held, own_half):
    c, xl, y = coordinates("core", "xl", "y")
    m = (c + (0 if own_half else 1)) % 2
    return [held.at[m, (xl + dxl) % 2 * 4 + (y + NY - dy) % NY] for dy in range(NY) for dxl in range(2)]


def ring_places(weight):
    (z,) = coordinates("z")
    starts = [(z + 8 + far) % 8 * 256 + 128 * (k == 8) for k, far in enumerate(RING)]
    return [weight.at[pl.ds(pl.multiple_of(at, 128), 256 if k < 7 else 128)] for k, at in enumerate(starts)]


def save_body(own, *refs):
    blocks, (held, weight, sems) = refs[:5], refs[5:]
    copies = []
    for k, place in enumerate(own_places(held, True)):
        copies.append(pltpu.make_async_copy(own.at[k // 2, k % 2], place, sems.at[k]))
    for k, place in enumerate(ring_places(weight)[:5]):
        copies.append(pltpu.make_async_copy(blocks[k], place, sems.at[8 + k]))
    for copy in copies:
        copy.start()
    for copy in copies:
        copy.wait()


def project_body(held_in, weight_in, own, other, *refs):
    blocks, (held, weight_out, out, weight, result, sems) = refs[:9], refs[9:]
    c, xl, y = coordinates("core", "xl", "y")
    copies = []
    for k, place in enumerate(ring_places(weight_out)[5:]):
        copies.append(pltpu.make_async_copy(blocks[5 + k], place, sems.at[8 + k]))
    for k, place in enumerate(own_places(held, False)):
        copies.append(pltpu.make_async_copy(other.at[k // 2, k % 2], place, sems.at[k]))
    for copy in copies:
        copy.start()
    for block, place in zip(blocks, ring_places(weight)):
        place[...] = block[...]
    for i, rows in enumerate((own, other)):
        result[...] = jnp.dot(rows[...].reshape(256, D), weight[...], preferred_element_type=F32).astype(BF)
        for dy in range(NY):
            for dxl in range(2):
                place = (c + i) % 2 * 8 + (xl + dxl) % 2 * 4 + (y + NY - dy) % NY
                row = (dy * 2 + dxl) * 32
                out[place] = result[row : row + 32, :]
    for copy in copies:
        copy.wait()


def decoder_body(lengths, own, other, stream_in, upstream, query_gains, keep, send, gain_parts,
                 pairs, streams, queries, softmax, incoming, gradients):
    xh, c = coordinates("xh", "core")
    for i in range(2):
        pairs[2 * i + c] = own[8 * i : 8 * i + 8]
        pairs[2 * i + 1 - c] = other[8 * i : 8 * i + 8]
    streams[0] = stream_in[...]
    incoming[...] = upstream[...].astype(F32)
    length = lengths[0, xh]
    block = (lax.broadcasted_iota(jnp.int32, (128, 256), 0) // 32) == (
        lax.broadcasted_iota(jnp.int32, (128, 256), 1) // HEAD)
    block = jnp.where(block, 1.0, 0.0).astype(BF)
    lane = lax.broadcasted_iota(jnp.int32, (ROWS, 256), 1)
    visible = lax.broadcasted_iota(jnp.int32, (ENC, 1024), 0) < length
    scale = HEAD**-0.5
    def spread(part):
        return jnp.concatenate([part] * 4, axis=0) * block
    def fold(part):
        low = jnp.where(lane < 64, part[0:32], part[32:64])
        high = jnp.where(lane < 192, part[64:96], part[96:128])
        return jnp.where(lane < 128, low, high)
    def dot(a, b, dims):
        return lax.dot_general(a, b, (dims, ((), ())), preferred_element_type=F32)
    def col(g, base=0):
        return slice(base + g * 256, base + (g + 1) * 256)

    def lan(g):
        return slice(g * 128, (g + 1) * 128)

    def keys(layer, g):
        return pairs[layer, g // 2, :, col(g % 2)]

    def values(layer, g):
        return pairs[layer, 4 + g // 2, :, col(g % 2)]

    for layer in range(LAYERS):
        wide = streams[layer].astype(F32)
        factor = lax.rsqrt(jnp.mean(wide * wide, axis=-1, keepdims=True) + EPSILON)
        q = (wide * factor * query_gains[layer]).astype(BF)
        queries[layer] = q
        scores = jnp.concatenate([dot(keys(layer, g), spread(q[:, col(g)]), ((1,), (1,))) for g in range(GROUPS)], axis=1) * scale
        scores = jnp.where(visible, scores, -1e30)
        highest = jnp.max(scores, axis=0, keepdims=True)
        weights = jnp.where(visible, jnp.exp(scores - highest), 0.0)
        rows = weights / jnp.sum(weights, axis=0, keepdims=True)
        softmax[layer] = rows
        narrow = rows.astype(BF)
        ctx = [fold(dot(narrow[:, lan(g)], values(layer, g), ((0,), (0,)))) for g in range(GROUPS)]
        streams[layer + 1] = (wide + jnp.concatenate(ctx, axis=1)).astype(BF)
    for layer in reversed(range(LAYERS)):
        wide = streams[layer].astype(F32)
        factor = lax.rsqrt(jnp.mean(wide * wide, axis=-1, keepdims=True) + EPSILON)
        grad = incoming[...]
        narrow_grad = grad.astype(BF)
        rows = softmax[layer]
        narrow = rows.astype(BF)
        parts = []
        for g in range(GROUPS):
            heads = spread(narrow_grad[:, col(g)])
            parts.append(dot(values(layer, g), heads, ((1,), (1,))))
            gradients[layer, :, col(g, D)] = dot(narrow[:, lan(g)], heads, ((1,), (0,))).astype(BF)
        softmax_gradient = jnp.concatenate(parts, axis=1)
        ds = rows * (softmax_gradient - jnp.sum(rows * softmax_gradient, axis=0, keepdims=True))
        ds = ds.astype(BF)
        q = queries[layer]
        dq = []
        for g in range(GROUPS):
            dq.append(fold(dot(ds[:, lan(g)], keys(layer, g), ((0,), (0,)))))
            gradients[layer, :, col(g)] = (dot(ds[:, lan(g)], spread(q[:, col(g)]), ((1,), (0,))) * scale).astype(BF)
        gradient = jnp.concatenate(dq, axis=1) * scale
        scaled = gradient * query_gains[layer]
        mean = jnp.mean(scaled * wide, axis=-1, keepdims=True)
        incoming[...] = grad + factor * scaled - wide * (factor * factor * factor) * mean
        gain_parts[layer] = jnp.sum(gradient * wide * factor, axis=0, keepdims=True)
    for i in range(2):
        keep[i] = gradients[2 * i + c]
        send[i] = gradients[2 * i + 1 - c]


def join_body(keep, received, out):
    for xh in range(2):
        for k in range(8):
            span = slice(k * 512, (k + 1) * 512)
            total = keep[xh, :, span].astype(F32) + received[xh, :, span].astype(F32)
            out[xh * 8 + k] = total.astype(BF)


def high_low(part):
    high = part.astype(BF)
    return high, (part - high.astype(F32)).astype(BF)


def back_body(gradient, held_far, weight, gain_parts, keep, extra, send, terms, parts, rows, held, sem):
    (c,) = coordinates("core")
    copy = pltpu.make_async_copy(held_far, held, sem)
    copy.start()
    flat = gradient[...].reshape(512, 512)
    for q in range(4):
        span = slice(q * 512, (q + 1) * 512)
        terms[:, span] = lax.dot_general(flat, weight[span, :], (((1,), (1,)), ((), ())), preferred_element_type=F32)
    copy.wait()
    for m in range(2):
        for peer in range(8):
            place = (m * 8 + peer) * 32
            product = terms[place : place + 32, :] * held[m, peer].astype(F32)
            if place == 0:
                parts[...] = jnp.sum(product, axis=0, keepdims=True)
            else:
                parts[...] += jnp.sum(product, axis=0, keepdims=True)
            rows[place : place + 32, :] = jnp.broadcast_to(jnp.sum(product, axis=1, keepdims=True), (32, 128))
    row_sums = jnp.transpose(rows[...])[0:1, :]
    for parity, is_send in ((c, False), (1 - c, True)):
        extras = []
        for i in range(2):
            layer_gain = gain_parts[2 * i + parity]
            extras += [layer_gain[:, :1024], layer_gain[:, 1024:]]
        extras.append(
            jnp.concatenate([parts[:, lanes((2 * i + parity) * 512, 512)] for i in range(2)], axis=1)
        )
        extras.append(jnp.concatenate([row_sums, jnp.zeros((1, 512), F32)], axis=1))
        extras.append(jnp.zeros((2, 1024), F32))
        block = jnp.concatenate(extras, axis=0)
        for i in range(2):
            part = terms[:, lanes((2 * i + parity) * 512, 512)]
            if is_send:
                send[:512, i * 512 : (i + 1) * 512] = part.astype(BF)
            else:
                keep[:, i * 512 : (i + 1) * 512] = part
        if is_send:
            send[512:, :] = jnp.concatenate(high_low(block), axis=0)
        else:
            extra[...] = block


def merge_body(keep, extra, received, out):
    carried = received[512:, :].astype(F32)
    extras = extra[...] + carried[0:8] + carried[8:16]
    for xh in range(2):
        span = slice(xh * 512, (xh + 1) * 512)
        block = jnp.concatenate(
            [
                extras[2 * xh : 2 * xh + 1, :512],
                extras[2 * xh : 2 * xh + 1, 512:],
                extras[2 * xh + 1 : 2 * xh + 2, :512],
                extras[2 * xh + 1 : 2 * xh + 2, 512:],
                extras[4:5, span],
                extras[5:6, :512],
                jnp.zeros((2, 512), F32),
            ],
            axis=0,
        )
        block = jnp.concatenate(high_low(block), axis=0)
        for k in range(8):
            for m in range(2):
                place = (m * 8 + k) * 32
                part = keep[place : place + 32, span] + received[place : place + 32, span].astype(F32)
                out[xh * 8 + k, m * 32 : (m + 1) * 32, :] = part.astype(BF)
            out[xh * 8 + k, 64:, :] = block


def finish_body(received, states, factor, final_gain, gradient, sums, rows):
    xl, y = coordinates("xl", "y")
    total = received[0].astype(F32)
    for k in range(1, 16):
        total += received[k].astype(F32)
    extras = total[64:72] + total[72:80]
    sums[...] = jnp.broadcast_to(extras[None], (8, 8, 512))
    rows[...] = jnp.transpose(jnp.broadcast_to(extras[5:6], (128, 512)))
    for m in range(2):
        span = slice(m * 32, (m + 1) * 32)
        row_sum = rows[lanes(m * 256 + (xl * 4 + y) * 32, 32), 0:1]
        scale = factor[span, 0:1]
        scaled = total[span] * final_gain[...]
        wide = states[span, :].astype(F32)
        gradient[span, :] = scale * scaled - wide * (scale * scale * (row_sum / D))


def close_body(received, final_gain, final_gradient, layers_gradient):
    total = received[0]
    for k in range(1, 8):
        total += received[k]
    for i in range(4):
        layers_gradient[:, i * 512 : (i + 1) * 512] = total[i : i + 1]
    final_gradient[...] = total[4:5] / final_gain[...]


def per_device(
    encoder_states, encoder_lengths, final_gain, decoder_states, query_gain, cross_weight, upstream
):
    states = encoder_states.reshape(64, 512)
    columns, pack, gain_row = kernel_call(
        pack_body,
        (cross_weight, states, final_gain, query_gain),
        [((8, 32, 512), BF), ((80, 512), BF), ((1, 512), F32)],
        [((512,), BF), ((1, D), BF), pltpu.SemaphoreType.DMA((11,))],
        far=(0, 1, 2, 3),
    )
    block = lax.all_to_all(columns, ("xl", "y"), 0, 0, tiled=True).reshape(256, 512)
    packs = [pack, shift(pack, core=1), shift(pack, xh=1), shift(pack, xh=1, core=1)]
    tile = ((256, 512), BF)
    half, factor, query_gains, stream, incoming, ahead1, behind1 = kernel_call(
        norm_body,
        packs + [shift(block, z=1), shift(block, z=-1), decoder_states, upstream],
        [((32, D), BF), ((64, 128), F32), ((4, 1, D), F32), ((ROWS, D), BF), ((ROWS, D), BF), tile, tile],
        [((64, D), F32), ((1, D), F32), pltpu.SemaphoreType.DMA((2,))],
        far=(6, 7),
        aliases={4: 5, 5: 6},
    )
    near, others, across, ahead2, behind2 = kernel_call(
        near_body,
        [shift(half, xl=1), half]
        + [shift(half, y=dy) for dy in range(1, NY)]
        + [shift(ahead1, z=1), shift(behind1, z=-1)],
        [((NY, 32, D), BF), ((NY - 1, 32, D), BF), ((32, D), BF), tile, tile],
        aliases={0: 2, 5: 3, 6: 4},
    )
    own_rows, upper, lower, ahead3, behind3 = kernel_call(
        group_body,
        [near, across, shift(others, xl=1), shift(ahead2, z=1), shift(behind2, z=-1)],
        [((NY, 2, 32, D), BF), ((128, 512), BF), ((128, 512), BF), tile, tile],
        aliases={3: 3, 4: 4},
    )
    ring = [block, ahead1, behind1, ahead2, behind2, ahead3, behind3, shift(upper, z=1), shift(lower, z=-1)]
    held, weight = kernel_call(
        save_body,
        [own_rows] + ring[:5],
        [((2, 8, 32, D), BF), ((D, 512), BF)],
        [pltpu.SemaphoreType.DMA((13,))],
        far_outs=(0, 1),
    )
    held, weight, projected = kernel_call(
        project_body,
        [held, weight, own_rows, shift(own_rows, core=1)] + ring,
        [((2, 8, 32, D), BF), ((D, 512), BF), ((16, 32, 512), BF)],
        [((D, 512), BF), ((256, 512), BF), pltpu.SemaphoreType.DMA((12,))],
        far=(0, 1),
        far_outs=(0, 1),
        near_outs=(2,),
        aliases={0: 0, 1: 1},
    )
    own_pairs = lax.all_to_all(projected, ("xh", "xl", "y"), 0, 0, tiled=True)
    other_pairs = shift(own_pairs, core=1)
    keep, send, gain_parts = kernel_call(
        decoder_body,
        (encoder_lengths.T, own_pairs, other_pairs, stream, incoming, query_gains),
        [((2, 32, 4096), BF), ((2, 32, 4096), BF), ((4, 1, D), F32)],
        [
            ((4, 8, 32, 512), BF),
            ((5, ROWS, D), BF),
            ((4, ROWS, D), BF),
            ((4, ENC, 1024), F32),
            ((ROWS, D), F32),
            ((4, 32, 4096), BF),
        ],
        scalars=1,
    )
    (joined,) = kernel_call(join_body, (keep, shift(send, core=1)), [((16, 32, 512), BF)], near_outs=(0,))
    joined = lax.all_to_all(joined, ("xh", "xl", "y"), 0, 0, tiled=True)
    term_keep, extra, term_send = kernel_call(
        back_body,
        (joined, held, weight, gain_parts),
        [((512, 1024), F32), ((8, 1024), F32), ((528, 1024), BF)],
        [
            ((512, D), F32),
            ((1, D), F32),
            ((512, 128), F32),
            ((2, 8, 32, D), BF),
            pltpu.SemaphoreType.DMA,
        ],
        far=(1,),
        near_outs=(0, 1, 2),
    )
    (merged,) = kernel_call(
        merge_body, (term_keep, extra, shift(term_send, core=1)), [((16, 80, 512), BF)], near_outs=(0,)
    )
    merged = lax.all_to_all(merged, ("xh", "xl", "y"), 0, 0, tiled=True)
    gradient, sums = kernel_call(
        finish_body,
        (merged, pack, factor, gain_row),
        [((64, 512), F32), ((8, 8, 512), F32)],
        [((512, 128), F32)],
        near_outs=(1,),
    )
    sums = lax.all_to_all(sums, "z", 0, 0, tiled=True)
    final_gradient, layers_gradient = kernel_call(
        close_body, (sums, gain_row), [((1, 512), F32), ((1, D), F32)]
    )
    return (gradient.reshape(2, 32, 512), final_gradient[0], layers_gradient)


def solution(mesh):
    dp, section = ("z", "xl", "y"), ("xh", "core")
    return jax.shard_map(
        per_device,
        mesh=Mesh(mesh.devices.reshape(SIZES), AXES),
        in_specs=(
            P(None, dp, section),
            P(None, dp),
            P(section),
            P(None, dp, None),
            P(section, None),
            P(section, dp, None),
            P(None, dp, None),
        ),
        out_specs=(P(None, dp, section), P(section), P(section, None)),
        check_vma=False,
    )
```

```python
import jax
import jax.numpy as jnp
import numpy as np
from jax import lax
from jax.experimental import pallas as pl
from jax.experimental.pallas import tpu as pltpu
from jax.sharding import Mesh
from jax.sharding import PartitionSpec as P

D = 2048
HEAD = 64
ENC = 32
ROWS = 32
LAYERS = 4
GROUPS = 8
EPSILON = 1e-06
AXES = ("xh", "core", "z", "xl", "y")
SIZES = (2, 2, 8, 2, 4)
NY = 4
BF, F32 = jnp.bfloat16, jnp.float32
MIB = 1 << 20


def shift(block, **moves):
    pairs = []
    for index in np.ndindex(*SIZES):
        to = list(index)
        for axis, by in moves.items():
            k = AXES.index(axis)
            to[k] = (index[k] + by) % SIZES[k] if axis in "yz" else index[k] ^ by
        pairs.append((int(np.ravel_multi_index(index, SIZES)), int(np.ravel_multi_index(to, SIZES))))
    return lax.ppermute(block, AXES, pairs)


def kernel_call(body, operands, outs, scratch=(), scalars=0, far=(), far_outs=(), near_outs=(), aliases=None, limit=16):
    operands = [
        pltpu.with_memory_space_constraint(x, pltpu.HBM) if i in far else x for i, x in enumerate(operands)
    ]
    spaces = [pltpu.SMEM if i < scalars else pltpu.HBM if i in far else pltpu.VMEM for i in range(len(operands))]
    return pl.pallas_call(
        body,
        out_shape=[
            pltpu.HBM(s, d) if i in far_outs else pltpu.VMEM(s, d) if i in near_outs else jax.ShapeDtypeStruct(s, d)
            for i, (s, d) in enumerate(outs)
        ],
        in_specs=[pl.BlockSpec(memory_space=space) for space in spaces],
        out_specs=[pl.BlockSpec(memory_space=pltpu.HBM if i in far_outs else pltpu.VMEM) for i in range(len(outs))],
        scratch_shapes=[pltpu.VMEM(*x) if isinstance(x, tuple) else x for x in scratch],
        input_output_aliases=aliases or {},
        compiler_params=pltpu.CompilerParams(vmem_limit_bytes=limit * MIB),
    )(*operands)


def coordinates(*axes):
    return tuple(lax.axis_index(axis) for axis in axes)


def lanes(start, size):
    return pl.ds(pl.multiple_of(start, size), size)


RING = (0, -1, 1, -2, 2, -3, 3, -4, -4)


def pack_body(weight, states, final_gain, query_gain, columns, pack, gain_row, gain, query, sems):
    copies = [
        pltpu.make_async_copy(states, pack.at[pl.ds(0, 64)], sems.at[8]),
        pltpu.make_async_copy(final_gain, gain, sems.at[9]),
        pltpu.make_async_copy(query_gain, query, sems.at[10]),
    ]
    for k in range(8):
        part = weight.at[0, :, pl.ds(k * 512, 512)]
        copies.append(pltpu.make_async_copy(part, columns.at[k], sems.at[k]))
    for copy in copies:
        copy.start()
    copies[1].wait()
    copies[2].wait()
    gain_row[...] = gain[...].astype(F32).reshape(1, 512)
    gains = [gain_row[...]]
    gains += [query[:, i * 512 : (i + 1) * 512].astype(F32) for i in range(4)]
    gains += [jnp.zeros((11, 512), F32)]
    pack[64:, :] = jnp.concatenate(gains, axis=0).astype(BF)
    copies[0].wait()
    for copy in copies[3:]:
        copy.wait()


def norm_body(p0, p1, p2, p3, ahead_in, behind_in, streams, upstreams,
              half, factor, query_gains, stream, upstream, ahead, behind, wide, final_gains, sems):
    xh, c = coordinates("xh", "core")
    mine = pl.ds(pl.multiple_of(c * ROWS, ROWS), ROWS)
    copies = [
        pltpu.make_async_copy(streams.at[xh, mine], stream, sems.at[0]),
        pltpu.make_async_copy(upstreams.at[xh, mine], upstream, sems.at[1]),
    ]
    for copy in copies:
        copy.start()
    section = xh * 2 + c
    for j, pack in enumerate((p0, p1, p2, p3)):
        peer = section ^ j
        wide[:, lanes(peer * 512, 512)] = pack[:64, :].astype(F32)
        gains = pack[64:, :].astype(F32)
        final_gains[:, lanes(peer * 512, 512)] = gains[0:1]
        for i in range(4):
            query_gains[peer, :, i * 512 : (i + 1) * 512] = gains[1 + i : 2 + i]
    states = wide[...]
    scale = lax.rsqrt(jnp.mean(states * states, axis=-1, keepdims=True) + EPSILON)
    factor[...] = jnp.broadcast_to(scale, (64, 128))
    wide[...] = states * scale * final_gains[...]
    half[...] = wide[lanes(c * 32, 32), :].astype(BF)
    for copy in copies:
        copy.wait()


def near_body(across_in, half, p1, p2, p3, ahead_in, behind_in, near, others, across, ahead, behind):
    near[0] = half[...]
    for k, part in enumerate((p1, p2, p3)):
        near[k + 1] = part[...]
        others[k] = part[...]


def group_body(near, across, beyond, ahead_in, behind_in, rows, upper, lower, ahead, behind):
    rows[0, 1] = across[...]
    for k in range(NY):
        rows[k, 0] = near[k]
        if k:
            rows[k, 1] = beyond[k - 1]
    upper[...] = ahead_in[:128]
    lower[...] = behind_in[128:]


def own_places(held, own_half):
    c, xl, y = coordinates("core", "xl", "y")
    m = (c + (0 if own_half else 1)) % 2
    return [held.at[m, (xl + dxl) % 2 * 4 + (y + NY - dy) % NY] for dy in range(NY) for dxl in range(2)]


def ring_places(weight):
    (z,) = coordinates("z")
    starts = [(z + 8 + far) % 8 * 256 + 128 * (k == 8) for k, far in enumerate(RING)]
    return [weight.at[pl.ds(pl.multiple_of(at, 128), 256 if k < 7 else 128)] for k, at in enumerate(starts)]


def save_body(own, *refs):
    blocks, (held, weight, sems) = refs[:5], refs[5:]
    copies = []
    for k, place in enumerate(own_places(held, True)):
        copies.append(pltpu.make_async_copy(own.at[k // 2, k % 2], place, sems.at[k]))
    for k, place in enumerate(ring_places(weight)[:5]):
        copies.append(pltpu.make_async_copy(blocks[k], place, sems.at[8 + k]))
    for copy in copies:
        copy.start()
    for copy in copies:
        copy.wait()


def project_body(held_in, weight_in, own, other, *refs):
    blocks, (held, weight_out, out, weight, result, sems) = refs[:9], refs[9:]
    c, xl, y = coordinates("core", "xl", "y")
    copies = []
    for k, place in enumerate(ring_places(weight_out)[5:]):
        copies.append(pltpu.make_async_copy(blocks[5 + k], place, sems.at[8 + k]))
    for k, place in enumerate(own_places(held, False)):
        copies.append(pltpu.make_async_copy(other.at[k // 2, k % 2], place, sems.at[k]))
    for copy in copies:
        copy.start()
    for block, place in zip(blocks, ring_places(weight)):
        place[...] = block[...]
    for i, rows in enumerate((own, other)):
        result[...] = jnp.dot(rows[...].reshape(256, D), weight[...], preferred_element_type=F32).astype(BF)
        for dy in range(NY):
            for dxl in range(2):
                place = (c + i) % 2 * 8 + (xl + dxl) % 2 * 4 + (y + NY - dy) % NY
                row = (dy * 2 + dxl) * 32
                out[place] = result[row : row + 32, :]
    for copy in copies:
        copy.wait()


def decoder_body(lengths, own, other, stream_in, upstream, query_gains, keep, send, gain_parts,
                 pairs, streams, queries, softmax, incoming, gradients):
    xh, c = coordinates("xh", "core")
    for i in range(2):
        pairs[2 * i + c] = own[8 * i : 8 * i + 8]
        pairs[2 * i + 1 - c] = other[8 * i : 8 * i + 8]
    streams[0] = stream_in[...]
    incoming[...] = upstream[...].astype(F32)
    length = lengths[0, xh]
    block = (lax.broadcasted_iota(jnp.int32, (128, 256), 0) // 32) == (
        lax.broadcasted_iota(jnp.int32, (128, 256), 1) // HEAD)
    block = jnp.where(block, 1.0, 0.0).astype(BF)
    lane = lax.broadcasted_iota(jnp.int32, (ROWS, 256), 1)
    visible = lax.broadcasted_iota(jnp.int32, (ENC, 1024), 0) < length
    scale = HEAD**-0.5
    def spread(part):
        return jnp.concatenate([part] * 4, axis=0) * block
    def fold(part):
        low = jnp.where(lane < 64, part[0:32], part[32:64])
        high = jnp.where(lane < 192, part[64:96], part[96:128])
        return jnp.where(lane < 128, low, high)
    def dot(a, b, dims):
        return lax.dot_general(a, b, (dims, ((), ())), preferred_element_type=F32)
    def col(g, base=0):
        return slice(base + g * 256, base + (g + 1) * 256)

    def lan(g):
        return slice(g * 128, (g + 1) * 128)

    def keys(layer, g):
        return pairs[layer, g // 2, :, col(g % 2)]

    def values(layer, g):
        return pairs[layer, 4 + g // 2, :, col(g % 2)]

    for layer in range(LAYERS):
        wide = streams[layer].astype(F32)
        factor = lax.rsqrt(jnp.mean(wide * wide, axis=-1, keepdims=True) + EPSILON)
        q = (wide * factor * query_gains[layer]).astype(BF)
        queries[layer] = q
        scores = jnp.concatenate([dot(keys(layer, g), spread(q[:, col(g)]), ((1,), (1,))) for g in range(GROUPS)], axis=1) * scale
        scores = jnp.where(visible, scores, -1e30)
        highest = jnp.max(scores, axis=0, keepdims=True)
        weights = jnp.where(visible, jnp.exp(scores - highest), 0.0)
        rows = weights / jnp.sum(weights, axis=0, keepdims=True)
        softmax[layer] = rows
        narrow = rows.astype(BF)
        ctx = [fold(dot(narrow[:, lan(g)], values(layer, g), ((0,), (0,)))) for g in range(GROUPS)]
        streams[layer + 1] = (wide + jnp.concatenate(ctx, axis=1)).astype(BF)
    for layer in reversed(range(LAYERS)):
        wide = streams[layer].astype(F32)
        factor = lax.rsqrt(jnp.mean(wide * wide, axis=-1, keepdims=True) + EPSILON)
        grad = incoming[...]
        narrow_grad = grad.astype(BF)
        rows = softmax[layer]
        narrow = rows.astype(BF)
        parts = []
        for g in range(GROUPS):
            heads = spread(narrow_grad[:, col(g)])
            parts.append(dot(values(layer, g), heads, ((1,), (1,))))
            gradients[layer, :, col(g, D)] = dot(narrow[:, lan(g)], heads, ((1,), (0,))).astype(BF)
        softmax_gradient = jnp.concatenate(parts, axis=1)
        ds = rows * (softmax_gradient - jnp.sum(rows * softmax_gradient, axis=0, keepdims=True))
        ds = ds.astype(BF)
        q = queries[layer]
        dq = []
        for g in range(GROUPS):
            dq.append(fold(dot(ds[:, lan(g)], keys(layer, g), ((0,), (0,)))))
            gradients[layer, :, col(g)] = (dot(ds[:, lan(g)], spread(q[:, col(g)]), ((1,), (0,))) * scale).astype(BF)
        gradient = jnp.concatenate(dq, axis=1) * scale
        scaled = gradient * query_gains[layer]
        mean = jnp.mean(scaled * wide, axis=-1, keepdims=True)
        incoming[...] = grad + factor * scaled - wide * (factor * factor * factor) * mean
        gain_parts[layer] = jnp.sum(gradient * wide * factor, axis=0, keepdims=True)
    for i in range(2):
        keep[i] = gradients[2 * i + c]
        send[i] = gradients[2 * i + 1 - c]


def join_body(keep, received, out):
    for xh in range(2):
        for k in range(8):
            span = slice(k * 512, (k + 1) * 512)
            total = keep[xh, :, span].astype(F32) + received[xh, :, span].astype(F32)
            out[xh * 8 + k] = total.astype(BF)


def high_low(part):
    high = part.astype(BF)
    return high, (part - high.astype(F32)).astype(BF)


def back_body(gradient, held_far, weight, gain_parts, keep, extra, send, terms, parts, rows, held, sem):
    (c,) = coordinates("core")
    copy = pltpu.make_async_copy(held_far, held, sem)
    copy.start()
    flat = gradient[...].reshape(512, 512)
    for q in range(4):
        span = slice(q * 512, (q + 1) * 512)
        terms[:, span] = lax.dot_general(flat, weight[span, :], (((1,), (1,)), ((), ())), preferred_element_type=F32)
    copy.wait()
    for m in range(2):
        for peer in range(8):
            place = (m * 8 + peer) * 32
            product = terms[place : place + 32, :] * held[m, peer].astype(F32)
            if place == 0:
                parts[...] = jnp.sum(product, axis=0, keepdims=True)
            else:
                parts[...] += jnp.sum(product, axis=0, keepdims=True)
            rows[place : place + 32, :] = jnp.broadcast_to(jnp.sum(product, axis=1, keepdims=True), (32, 128))
    row_sums = jnp.transpose(rows[...])[0:1, :]
    for parity, is_send in ((c, False), (1 - c, True)):
        extras = []
        for i in range(2):
            layer_gain = gain_parts[2 * i + parity]
            extras += [layer_gain[:, :1024], layer_gain[:, 1024:]]
        extras.append(
            jnp.concatenate([parts[:, lanes((2 * i + parity) * 512, 512)] for i in range(2)], axis=1)
        )
        extras.append(jnp.concatenate([row_sums, jnp.zeros((1, 512), F32)], axis=1))
        extras.append(jnp.zeros((2, 1024), F32))
        block = jnp.concatenate(extras, axis=0)
        for i in range(2):
            part = terms[:, lanes((2 * i + parity) * 512, 512)]
            if is_send:
                send[:512, i * 512 : (i + 1) * 512] = part.astype(BF)
            else:
                keep[:, i * 512 : (i + 1) * 512] = part
        if is_send:
            send[512:, :] = jnp.concatenate(high_low(block), axis=0)
        else:
            extra[...] = block


def gains_body(extra, received, out):
    carried = received[512:, :].astype(F32)
    extras = extra[...] + carried[0:8] + carried[8:16]
    for xh in range(2):
        block = jnp.concatenate(
            [
                extras[2 * xh : 2 * xh + 1, :512],
                extras[2 * xh : 2 * xh + 1, 512:],
                extras[2 * xh + 1 : 2 * xh + 2, :512],
                extras[2 * xh + 1 : 2 * xh + 2, 512:],
                extras[4:5, xh * 512 : (xh + 1) * 512],
                extras[5:6, :512],
                jnp.zeros((2, 512), F32),
            ],
            axis=0,
        )
        for k in range(8):
            out[xh * 8 + k] = block


def merge_body(keep, received, gains, out, sums, row_sums):
    total = gains[0]
    for k in range(1, 16):
        total += gains[k]
    sums[...] = total
    row_sums[...] = total[5:6]
    for xh in range(2):
        span = slice(xh * 512, (xh + 1) * 512)
        for k in range(8):
            for m in range(2):
                place = (m * 8 + k) * 32
                part = keep[place : place + 32, span] + received[place : place + 32, span].astype(F32)
                out[xh * 8 + k, m * 32 : (m + 1) * 32, :] = part.astype(BF)


def finish_body(received, states, factor, final_gain, row_totals, first, second, third,
                gradient, final_gradient, layers_gradient, rows):
    xl, y = coordinates("xl", "y")
    sums = first[...] + second[...] + third[...]
    for i in range(4):
        layers_gradient[:, i * 512 : (i + 1) * 512] = sums[i : i + 1]
    final_gradient[...] = sums[4:5] / final_gain[...]
    total = received[0].astype(F32)
    for k in range(1, 16):
        total += received[k].astype(F32)
    rows[...] = jnp.transpose(jnp.broadcast_to(row_totals[...], (128, 512)))
    for m in range(2):
        span = slice(m * 32, (m + 1) * 32)
        row_sum = rows[lanes(m * 256 + (xl * 4 + y) * 32, 32), 0:1]
        scale = factor[span, 0:1]
        scaled = total[span] * final_gain[...]
        wide = states[span, :].astype(F32)
        gradient[span, :] = scale * scaled - wide * (scale * scale * (row_sum / D))


def per_device(
    encoder_states, encoder_lengths, final_gain, decoder_states, query_gain, cross_weight, upstream
):
    states = encoder_states.reshape(64, 512)
    columns, pack, gain_row = kernel_call(
        pack_body,
        (cross_weight, states, final_gain, query_gain),
        [((8, 32, 512), BF), ((80, 512), BF), ((1, 512), F32)],
        [((512,), BF), ((1, D), BF), pltpu.SemaphoreType.DMA((11,))],
        far=(0, 1, 2, 3),
    )
    block = lax.all_to_all(columns, ("xl", "y"), 0, 0, tiled=True).reshape(256, 512)
    packs = [pack, shift(pack, core=1), shift(pack, xh=1), shift(pack, xh=1, core=1)]
    tile = ((256, 512), BF)
    half, factor, query_gains, stream, incoming, ahead1, behind1 = kernel_call(
        norm_body,
        packs + [shift(block, z=1), shift(block, z=-1), decoder_states, upstream],
        [((32, D), BF), ((64, 128), F32), ((4, 1, D), F32), ((ROWS, D), BF), ((ROWS, D), BF), tile, tile],
        [((64, D), F32), ((1, D), F32), pltpu.SemaphoreType.DMA((2,))],
        far=(6, 7),
        aliases={4: 5, 5: 6},
    )
    near, others, across, ahead2, behind2 = kernel_call(
        near_body,
        [shift(half, xl=1), half]
        + [shift(half, y=dy) for dy in range(1, NY)]
        + [shift(ahead1, z=1), shift(behind1, z=-1)],
        [((NY, 32, D), BF), ((NY - 1, 32, D), BF), ((32, D), BF), tile, tile],
        aliases={0: 2, 5: 3, 6: 4},
    )
    own_rows, upper, lower, ahead3, behind3 = kernel_call(
        group_body,
        [near, across, shift(others, xl=1), shift(ahead2, z=1), shift(behind2, z=-1)],
        [((NY, 2, 32, D), BF), ((128, 512), BF), ((128, 512), BF), tile, tile],
        aliases={3: 3, 4: 4},
    )
    ring = [block, ahead1, behind1, ahead2, behind2, ahead3, behind3, shift(upper, z=1), shift(lower, z=-1)]
    held, weight = kernel_call(
        save_body,
        [own_rows] + ring[:5],
        [((2, 8, 32, D), BF), ((D, 512), BF)],
        [pltpu.SemaphoreType.DMA((13,))],
        far_outs=(0, 1),
    )
    held, weight, projected = kernel_call(
        project_body,
        [held, weight, own_rows, shift(own_rows, core=1)] + ring,
        [((2, 8, 32, D), BF), ((D, 512), BF), ((16, 32, 512), BF)],
        [((D, 512), BF), ((256, 512), BF), pltpu.SemaphoreType.DMA((12,))],
        far=(0, 1),
        far_outs=(0, 1),
        near_outs=(2,),
        aliases={0: 0, 1: 1},
    )
    own_pairs = lax.all_to_all(projected, ("xh", "xl", "y"), 0, 0, tiled=True)
    other_pairs = shift(own_pairs, core=1)
    keep, send, gain_parts = kernel_call(
        decoder_body,
        (encoder_lengths.T, own_pairs, other_pairs, stream, incoming, query_gains),
        [((2, 32, 4096), BF), ((2, 32, 4096), BF), ((4, 1, D), F32)],
        [
            ((4, 8, 32, 512), BF),
            ((5, ROWS, D), BF),
            ((4, ROWS, D), BF),
            ((4, ENC, 1024), F32),
            ((ROWS, D), F32),
            ((4, 32, 4096), BF),
        ],
        scalars=1,
    )
    (joined,) = kernel_call(join_body, (keep, shift(send, core=1)), [((16, 32, 512), BF)], near_outs=(0,))
    joined = lax.all_to_all(joined, ("xh", "xl", "y"), 0, 0, tiled=True)
    term_keep, extra, term_send = kernel_call(
        back_body,
        (joined, held, weight, gain_parts),
        [((512, 1024), F32), ((8, 1024), F32), ((528, 1024), BF)],
        [
            ((512, D), F32),
            ((1, D), F32),
            ((512, 128), F32),
            ((2, 8, 32, D), BF),
            pltpu.SemaphoreType.DMA,
        ],
        far=(1,),
        near_outs=(0, 1, 2),
    )
    received = shift(term_send, core=1)
    (gains,) = kernel_call(gains_body, (extra, received), [((16, 8, 512), F32)], near_outs=(0,))
    gains = lax.all_to_all(gains, ("xh", "xl", "y"), 0, 0, tiled=True)
    merged, sums, row_sums = kernel_call(
        merge_body,
        (term_keep, received, gains),
        [((16, 64, 512), BF), ((8, 512), F32), ((1, 512), F32)],
        near_outs=(0,),
    )
    merged = lax.all_to_all(merged, ("xh", "xl", "y"), 0, 0, tiled=True)
    pair = sums + shift(sums, z=1)
    triple = pair + shift(sums, z=-1)
    gradient, final_gradient, layers_gradient = kernel_call(
        finish_body,
        (merged, pack, factor, gain_row, row_sums, triple, shift(triple, z=-3), shift(pair, z=2)),
        [((64, 512), F32), ((1, 512), F32), ((1, D), F32)],
        [((512, 128), F32)],
    )
    return (gradient.reshape(2, 32, 512), final_gradient[0], layers_gradient)


def solution(mesh):
    dp, section = ("z", "xl", "y"), ("xh", "core")
    return jax.shard_map(
        per_device,
        mesh=Mesh(mesh.devices.reshape(SIZES), AXES),
        in_specs=(
            P(None, dp, section),
            P(None, dp),
            P(section),
            P(None, dp, None),
            P(section, None),
            P(section, dp, None),
            P(None, dp, None),
        ),
        out_specs=(P(None, dp, section), P(section), P(section, None)),
        check_vma=False,
    )
```

```python
import jax
import jax.numpy as jnp
import numpy as np
from jax import lax
from jax.experimental import pallas as pl
from jax.experimental.pallas import tpu as pltpu
from jax.sharding import Mesh
from jax.sharding import PartitionSpec as P

D = 2048
HEAD = 64
ENC = 32
ROWS = 32
LAYERS = 4
GROUPS = 8
EPSILON = 1e-06
AXES = ("xh", "core", "z", "xl", "y")
SIZES = (2, 2, 8, 2, 4)
NY = 4
BF, F32 = jnp.bfloat16, jnp.float32
MIB = 1 << 20


def shift(block, **moves):
    pairs = []
    for index in np.ndindex(*SIZES):
        to = list(index)
        for axis, by in moves.items():
            k = AXES.index(axis)
            to[k] = (index[k] + by) % SIZES[k] if axis in "yz" else index[k] ^ by
        pairs.append((int(np.ravel_multi_index(index, SIZES)), int(np.ravel_multi_index(to, SIZES))))
    return lax.ppermute(block, AXES, pairs)


def kernel_call(body, operands, outs, scratch=(), scalars=0, far=(), far_outs=(), near_outs=(), aliases=None, limit=16):
    operands = [
        pltpu.with_memory_space_constraint(x, pltpu.HBM) if i in far else x for i, x in enumerate(operands)
    ]
    spaces = [pltpu.SMEM if i < scalars else pltpu.HBM if i in far else pltpu.VMEM for i in range(len(operands))]
    return pl.pallas_call(
        body,
        out_shape=[
            pltpu.HBM(s, d) if i in far_outs else pltpu.VMEM(s, d) if i in near_outs else jax.ShapeDtypeStruct(s, d)
            for i, (s, d) in enumerate(outs)
        ],
        in_specs=[pl.BlockSpec(memory_space=space) for space in spaces],
        out_specs=[pl.BlockSpec(memory_space=pltpu.HBM if i in far_outs else pltpu.VMEM) for i in range(len(outs))],
        scratch_shapes=[pltpu.VMEM(*x) if isinstance(x, tuple) else x for x in scratch],
        input_output_aliases=aliases or {},
        compiler_params=pltpu.CompilerParams(vmem_limit_bytes=limit * MIB),
    )(*operands)


def coordinates(*axes):
    return tuple(lax.axis_index(axis) for axis in axes)


def lanes(start, size):
    return pl.ds(pl.multiple_of(start, size), size)


RING = (0, -1, 1, -2, 2, -3, 3, -4, -4)


def pack_body(weight, states, final_gain, query_gain, columns, pack, gain_row, gain, query, sems):
    copies = [
        pltpu.make_async_copy(states, pack.at[pl.ds(0, 64)], sems.at[8]),
        pltpu.make_async_copy(final_gain, gain, sems.at[9]),
        pltpu.make_async_copy(query_gain, query, sems.at[10]),
    ]
    for k in range(8):
        part = weight.at[0, :, pl.ds(k * 512, 512)]
        copies.append(pltpu.make_async_copy(part, columns.at[k], sems.at[k]))
    for copy in copies:
        copy.start()
    copies[1].wait()
    copies[2].wait()
    gain_row[...] = gain[...].astype(F32).reshape(1, 512)
    gains = [gain_row[...]]
    gains += [query[:, i * 512 : (i + 1) * 512].astype(F32) for i in range(4)]
    gains += [jnp.zeros((11, 512), F32)]
    pack[64:, :] = jnp.concatenate(gains, axis=0).astype(BF)
    copies[0].wait()
    for copy in copies[3:]:
        copy.wait()


def norm_body(p0, p1, p2, p3, ahead_in, behind_in, streams, upstreams,
              half, factor, query_gains, stream, upstream, ahead, behind, wide, final_gains, sems):
    xh, c = coordinates("xh", "core")
    mine = pl.ds(pl.multiple_of(c * ROWS, ROWS), ROWS)
    copies = [
        pltpu.make_async_copy(streams.at[xh, mine], stream, sems.at[0]),
        pltpu.make_async_copy(upstreams.at[xh, mine], upstream, sems.at[1]),
    ]
    for copy in copies:
        copy.start()
    section = xh * 2 + c
    for j, pack in enumerate((p0, p1, p2, p3)):
        peer = section ^ j
        wide[:, lanes(peer * 512, 512)] = pack[:64, :].astype(F32)
        gains = pack[64:, :].astype(F32)
        final_gains[:, lanes(peer * 512, 512)] = gains[0:1]
        for i in range(4):
            query_gains[peer, :, i * 512 : (i + 1) * 512] = gains[1 + i : 2 + i]
    states = wide[...]
    scale = lax.rsqrt(jnp.mean(states * states, axis=-1, keepdims=True) + EPSILON)
    factor[...] = jnp.broadcast_to(scale, (64, 128))
    wide[...] = states * scale * final_gains[...]
    half[...] = wide[lanes(c * 32, 32), :].astype(BF)
    for copy in copies:
        copy.wait()


def near_body(across_in, half, p1, p2, p3, ahead_in, behind_in, near, others, across, ahead, behind):
    near[0] = half[...]
    for k, part in enumerate((p1, p2, p3)):
        near[k + 1] = part[...]
        others[k] = part[...]


def group_body(near, across, beyond, ahead_in, behind_in, rows, upper, lower, ahead, behind):
    rows[0, 1] = across[...]
    for k in range(NY):
        rows[k, 0] = near[k]
        if k:
            rows[k, 1] = beyond[k - 1]
    upper[...] = ahead_in[:128]
    lower[...] = behind_in[128:]


def own_places(held, own_half):
    c, xl, y = coordinates("core", "xl", "y")
    m = (c + (0 if own_half else 1)) % 2
    return [held.at[m, (xl + dxl) % 2 * 4 + (y + NY - dy) % NY] for dy in range(NY) for dxl in range(2)]


def ring_places(weight):
    (z,) = coordinates("z")
    starts = [(z + 8 + far) % 8 * 256 + 128 * (k == 8) for k, far in enumerate(RING)]
    return [weight.at[pl.ds(pl.multiple_of(at, 128), 256 if k < 7 else 128)] for k, at in enumerate(starts)]


def save_body(own, *refs):
    blocks, (held, weight, sems) = refs[:5], refs[5:]
    copies = []
    for k, place in enumerate(own_places(held, True)):
        copies.append(pltpu.make_async_copy(own.at[k // 2, k % 2], place, sems.at[k]))
    for k, place in enumerate(ring_places(weight)[:5]):
        copies.append(pltpu.make_async_copy(blocks[k], place, sems.at[8 + k]))
    for copy in copies:
        copy.start()
    for copy in copies:
        copy.wait()


def project_body(held_in, weight_in, own, other, *refs):
    blocks, (held, weight_out, out, weight, result, sems) = refs[:9], refs[9:]
    c, xl, y = coordinates("core", "xl", "y")
    copies = []
    for k, place in enumerate(ring_places(weight_out)[5:]):
        copies.append(pltpu.make_async_copy(blocks[5 + k], place, sems.at[8 + k]))
    for k, place in enumerate(own_places(held, False)):
        copies.append(pltpu.make_async_copy(other.at[k // 2, k % 2], place, sems.at[k]))
    for copy in copies:
        copy.start()
    for block, place in zip(blocks, ring_places(weight)):
        place[...] = block[...]
    for i, rows in enumerate((own, other)):
        result[...] = jnp.dot(rows[...].reshape(256, D), weight[...], preferred_element_type=F32).astype(BF)
        for dy in range(NY):
            for dxl in range(2):
                place = (c + i) % 2 * 8 + (xl + dxl) % 2 * 4 + (y + NY - dy) % NY
                row = (dy * 2 + dxl) * 32
                out[place] = result[row : row + 32, :]
    for copy in copies:
        copy.wait()


def decoder_body(lengths, own, other, stream_in, upstream, query_gains, keep, send, gain_parts,
                 pairs, streams, queries, softmax, incoming, gradients):
    xh, c = coordinates("xh", "core")
    for i in range(2):
        pairs[2 * i + c] = own[8 * i : 8 * i + 8]
        pairs[2 * i + 1 - c] = other[8 * i : 8 * i + 8]
    streams[0] = stream_in[...]
    incoming[...] = upstream[...].astype(F32)
    length = lengths[0, xh]
    block = (lax.broadcasted_iota(jnp.int32, (128, 256), 0) // 32) == (
        lax.broadcasted_iota(jnp.int32, (128, 256), 1) // HEAD)
    block = jnp.where(block, 1.0, 0.0).astype(BF)
    lane = lax.broadcasted_iota(jnp.int32, (ROWS, 256), 1)
    visible = lax.broadcasted_iota(jnp.int32, (ENC, 1024), 0) < length
    scale = HEAD**-0.5
    def spread(part):
        return jnp.concatenate([part] * 4, axis=0) * block
    def fold(part):
        low = jnp.where(lane < 64, part[0:32], part[32:64])
        high = jnp.where(lane < 192, part[64:96], part[96:128])
        return jnp.where(lane < 128, low, high)
    def dot(a, b, dims):
        return lax.dot_general(a, b, (dims, ((), ())), preferred_element_type=F32)
    def col(g, base=0):
        return slice(base + g * 256, base + (g + 1) * 256)

    def lan(g):
        return slice(g * 128, (g + 1) * 128)

    def keys(layer, g):
        return pairs[layer, g // 2, :, col(g % 2)]

    def values(layer, g):
        return pairs[layer, 4 + g // 2, :, col(g % 2)]

    for layer in range(LAYERS):
        wide = streams[layer].astype(F32)
        factor = lax.rsqrt(jnp.mean(wide * wide, axis=-1, keepdims=True) + EPSILON)
        q = (wide * factor * query_gains[layer]).astype(BF)
        queries[layer] = q
        scores = jnp.concatenate([dot(keys(layer, g), spread(q[:, col(g)]), ((1,), (1,))) for g in range(GROUPS)], axis=1) * scale
        scores = jnp.where(visible, scores, -1e30)
        highest = jnp.max(scores, axis=0, keepdims=True)
        weights = jnp.where(visible, jnp.exp(scores - highest), 0.0)
        rows = weights / jnp.sum(weights, axis=0, keepdims=True)
        softmax[layer] = rows
        narrow = rows.astype(BF)
        ctx = [fold(dot(narrow[:, lan(g)], values(layer, g), ((0,), (0,)))) for g in range(GROUPS)]
        streams[layer + 1] = (wide + jnp.concatenate(ctx, axis=1)).astype(BF)
    for layer in reversed(range(LAYERS)):
        wide = streams[layer].astype(F32)
        factor = lax.rsqrt(jnp.mean(wide * wide, axis=-1, keepdims=True) + EPSILON)
        grad = incoming[...]
        narrow_grad = grad.astype(BF)
        rows = softmax[layer]
        narrow = rows.astype(BF)
        parts = []
        for g in range(GROUPS):
            heads = spread(narrow_grad[:, col(g)])
            parts.append(dot(values(layer, g), heads, ((1,), (1,))))
            gradients[layer, :, col(g, D)] = dot(narrow[:, lan(g)], heads, ((1,), (0,))).astype(BF)
        softmax_gradient = jnp.concatenate(parts, axis=1)
        ds = rows * (softmax_gradient - jnp.sum(rows * softmax_gradient, axis=0, keepdims=True))
        ds = ds.astype(BF)
        q = queries[layer]
        dq = []
        for g in range(GROUPS):
            dq.append(fold(dot(ds[:, lan(g)], keys(layer, g), ((0,), (0,)))))
            gradients[layer, :, col(g)] = (dot(ds[:, lan(g)], spread(q[:, col(g)]), ((1,), (0,))) * scale).astype(BF)
        gradient = jnp.concatenate(dq, axis=1) * scale
        scaled = gradient * query_gains[layer]
        mean = jnp.mean(scaled * wide, axis=-1, keepdims=True)
        incoming[...] = grad + factor * scaled - wide * (factor * factor * factor) * mean
        gain_parts[layer] = jnp.sum(gradient * wide * factor, axis=0, keepdims=True)
    for i in range(2):
        keep[i] = gradients[2 * i + c]
        send[i] = gradients[2 * i + 1 - c]


def join_body(keep, received, out):
    for xh in range(2):
        for k in range(8):
            span = slice(k * 512, (k + 1) * 512)
            total = keep[xh, :, span].astype(F32) + received[xh, :, span].astype(F32)
            out[xh * 8 + k] = total.astype(BF)


def back_body(gradient, held_far, weight, gain_parts, keep, extra, extra_send, send, terms, parts, rows, held, sem):
    (c,) = coordinates("core")
    copy = pltpu.make_async_copy(held_far, held, sem)
    copy.start()
    flat = gradient[...].reshape(512, 512)
    for q in range(4):
        span = slice(q * 512, (q + 1) * 512)
        terms[:, span] = lax.dot_general(flat, weight[span, :], (((1,), (1,)), ((), ())), preferred_element_type=F32)
    copy.wait()
    for m in range(2):
        for peer in range(8):
            place = (m * 8 + peer) * 32
            product = terms[place : place + 32, :] * held[m, peer].astype(F32)
            if place == 0:
                parts[...] = jnp.sum(product, axis=0, keepdims=True)
            else:
                parts[...] += jnp.sum(product, axis=0, keepdims=True)
            rows[place : place + 32, :] = jnp.broadcast_to(jnp.sum(product, axis=1, keepdims=True), (32, 128))
    row_sums = jnp.transpose(rows[...])[0:1, :]
    for parity, is_send in ((c, False), (1 - c, True)):
        extras = []
        for i in range(2):
            layer_gain = gain_parts[2 * i + parity]
            extras += [layer_gain[:, :1024], layer_gain[:, 1024:]]
        extras.append(
            jnp.concatenate([parts[:, lanes((2 * i + parity) * 512, 512)] for i in range(2)], axis=1)
        )
        extras.append(jnp.concatenate([row_sums, jnp.zeros((1, 512), F32)], axis=1))
        extras.append(jnp.zeros((2, 1024), F32))
        block = jnp.concatenate(extras, axis=0)
        for i in range(2):
            part = terms[:, lanes((2 * i + parity) * 512, 512)]
            if is_send:
                send[:, i * 512 : (i + 1) * 512] = part.astype(BF)
            else:
                keep[:, i * 512 : (i + 1) * 512] = part
        if is_send:
            extra_send[...] = block
        else:
            extra[...] = block


def flatten(block):
    return jnp.concatenate([block[i : i + 1] for i in range(8)], axis=1)


def gains_body(extra, received, out):
    extras = extra[...] + received[...]
    for xh in range(2):
        flat = jnp.concatenate(
            [
                extras[2 * xh : 2 * xh + 1],
                extras[2 * xh + 1 : 2 * xh + 2],
                extras[4:5, xh * 512 : (xh + 1) * 512],
                extras[5:6, :512],
            ],
            axis=1,
        )
        block = jnp.concatenate([flat[:, i * 384 : (i + 1) * 384] for i in range(8)], axis=0)
        for k in range(8):
            out[xh * 8 + k] = block


def merge_body(keep, received, gains, out, sums, row_sums):
    total = gains[0]
    for k in range(1, 16):
        total += gains[k]
    sums[...] = total
    row_sums[...] = flatten(total)[:, 2560:]
    for xh in range(2):
        span = slice(xh * 512, (xh + 1) * 512)
        for k in range(8):
            for m in range(2):
                place = (m * 8 + k) * 32
                part = keep[place : place + 32, span] + received[place : place + 32, span].astype(F32)
                out[xh * 8 + k, m * 32 : (m + 1) * 32, :] = part.astype(BF)


def finish_body(received, states, factor, final_gain, row_totals, first, second, third,
                gradient, final_gradient, layers_gradient, rows):
    xl, y = coordinates("xl", "y")
    sums = first[...] + second[...] + third[...]
    flat = flatten(sums)
    layers_gradient[...] = flat[:, :D]
    final_gradient[...] = flat[:, D:2560] / final_gain[...]
    total = received[0].astype(F32)
    for k in range(1, 16):
        total += received[k].astype(F32)
    rows[...] = jnp.transpose(jnp.broadcast_to(row_totals[...], (128, 512)))
    for m in range(2):
        span = slice(m * 32, (m + 1) * 32)
        row_sum = rows[lanes(m * 256 + (xl * 4 + y) * 32, 32), 0:1]
        scale = factor[span, 0:1]
        scaled = total[span] * final_gain[...]
        wide = states[span, :].astype(F32)
        gradient[span, :] = scale * scaled - wide * (scale * scale * (row_sum / D))


def per_device(
    encoder_states, encoder_lengths, final_gain, decoder_states, query_gain, cross_weight, upstream
):
    states = encoder_states.reshape(64, 512)
    columns, pack, gain_row = kernel_call(
        pack_body,
        (cross_weight, states, final_gain, query_gain),
        [((8, 32, 512), BF), ((80, 512), BF), ((1, 512), F32)],
        [((512,), BF), ((1, D), BF), pltpu.SemaphoreType.DMA((11,))],
        far=(0, 1, 2, 3),
    )
    block = lax.all_to_all(columns, ("xl", "y"), 0, 0, tiled=True).reshape(256, 512)
    packs = [pack, shift(pack, core=1), shift(pack, xh=1), shift(pack, xh=1, core=1)]
    tile = ((256, 512), BF)
    half, factor, query_gains, stream, incoming, ahead1, behind1 = kernel_call(
        norm_body,
        packs + [shift(block, z=1), shift(block, z=-1), decoder_states, upstream],
        [((32, D), BF), ((64, 128), F32), ((4, 1, D), F32), ((ROWS, D), BF), ((ROWS, D), BF), tile, tile],
        [((64, D), F32), ((1, D), F32), pltpu.SemaphoreType.DMA((2,))],
        far=(6, 7),
        aliases={4: 5, 5: 6},
    )
    near, others, across, ahead2, behind2 = kernel_call(
        near_body,
        [shift(half, xl=1), half]
        + [shift(half, y=dy) for dy in range(1, NY)]
        + [shift(ahead1, z=1), shift(behind1, z=-1)],
        [((NY, 32, D), BF), ((NY - 1, 32, D), BF), ((32, D), BF), tile, tile],
        aliases={0: 2, 5: 3, 6: 4},
    )
    own_rows, upper, lower, ahead3, behind3 = kernel_call(
        group_body,
        [near, across, shift(others, xl=1), shift(ahead2, z=1), shift(behind2, z=-1)],
        [((NY, 2, 32, D), BF), ((128, 512), BF), ((128, 512), BF), tile, tile],
        aliases={3: 3, 4: 4},
    )
    ring = [block, ahead1, behind1, ahead2, behind2, ahead3, behind3, shift(upper, z=1), shift(lower, z=-1)]
    held, weight = kernel_call(
        save_body,
        [own_rows] + ring[:5],
        [((2, 8, 32, D), BF), ((D, 512), BF)],
        [pltpu.SemaphoreType.DMA((13,))],
        far_outs=(0, 1),
    )
    held, weight, projected = kernel_call(
        project_body,
        [held, weight, own_rows, shift(own_rows, core=1)] + ring,
        [((2, 8, 32, D), BF), ((D, 512), BF), ((16, 32, 512), BF)],
        [((D, 512), BF), ((256, 512), BF), pltpu.SemaphoreType.DMA((12,))],
        far=(0, 1),
        far_outs=(0, 1),
        near_outs=(2,),
        aliases={0: 0, 1: 1},
    )
    own_pairs = lax.all_to_all(projected, ("xh", "xl", "y"), 0, 0, tiled=True)
    other_pairs = shift(own_pairs, core=1)
    keep, send, gain_parts = kernel_call(
        decoder_body,
        (encoder_lengths.T, own_pairs, other_pairs, stream, incoming, query_gains),
        [((2, 32, 4096), BF), ((2, 32, 4096), BF), ((4, 1, D), F32)],
        [
            ((4, 8, 32, 512), BF),
            ((5, ROWS, D), BF),
            ((4, ROWS, D), BF),
            ((4, ENC, 1024), F32),
            ((ROWS, D), F32),
            ((4, 32, 4096), BF),
        ],
        scalars=1,
    )
    (joined,) = kernel_call(join_body, (keep, shift(send, core=1)), [((16, 32, 512), BF)], near_outs=(0,))
    joined = lax.all_to_all(joined, ("xh", "xl", "y"), 0, 0, tiled=True)
    term_keep, extra, extra_send, term_send = kernel_call(
        back_body,
        (joined, held, weight, gain_parts),
        [((512, 1024), F32), ((8, 1024), F32), ((8, 1024), F32), ((512, 1024), BF)],
        [
            ((512, D), F32),
            ((1, D), F32),
            ((512, 128), F32),
            ((2, 8, 32, D), BF),
            pltpu.SemaphoreType.DMA,
        ],
        far=(1,),
        near_outs=(0, 1, 2, 3),
    )
    received = shift(term_send, core=1)
    (gains,) = kernel_call(gains_body, (extra, shift(extra_send, core=1)), [((16, 8, 384), F32)], near_outs=(0,))
    gains = lax.all_to_all(gains, ("xh", "xl", "y"), 0, 0, tiled=True)
    merged, sums, row_sums = kernel_call(
        merge_body,
        (term_keep, received, gains),
        [((16, 64, 512), BF), ((8, 384), F32), ((1, 512), F32)],
        near_outs=(0,),
    )
    merged = lax.all_to_all(merged, ("xh", "xl", "y"), 0, 0, tiled=True)
    pair = sums + shift(sums, z=1)
    triple = pair + shift(sums, z=-1)
    gradient, final_gradient, layers_gradient = kernel_call(
        finish_body,
        (merged, pack, factor, gain_row, row_sums, triple, shift(triple, z=-3), shift(pair, z=2)),
        [((64, 512), F32), ((1, 512), F32), ((1, D), F32)],
        [((512, 128), F32)],
    )
    return (gradient.reshape(2, 32, 512), final_gradient[0], layers_gradient)


def solution(mesh):
    dp, section = ("z", "xl", "y"), ("xh", "core")
    return jax.shard_map(
        per_device,
        mesh=Mesh(mesh.devices.reshape(SIZES), AXES),
        in_specs=(
            P(None, dp, section),
            P(None, dp),
            P(section),
            P(None, dp, None),
            P(section, None),
            P(section, dp, None),
            P(None, dp, None),
        ),
        out_specs=(P(None, dp, section), P(section), P(section, None)),
        check_vma=False,
    )
```
